128 devices in a mesh: table: 16 (over y, z), expert: 8 (over x, core).
Axes of the slice: x: 4, y: 4, z: 4, core: 2. Of those that a mesh axis runs over, the one named last changes fastest.
Arguments:
- emb_rows: bfloat16 [8192, 128], P('table'), may hold values from -3 to 3
- row_ids: int32 [16384, 8, 4], P(('table', 'expert')), may hold values from 0 to 8191
- route_ids: int32 [16384, 2], P(('table', 'expert')), may hold values from 0 to 7, all different within a row; in each aligned block of 128 rows (0 to 127, 128 to 255, ...) at most 48 rows name the same one
- route_gates: float32 [16384, 2], P(('table', 'expert')), may hold values from 0.1 to 1
- w_in: bfloat16 [8, 1024, 4096], P('expert'), may hold values from -0.1875 to 0.1875
- w_out: bfloat16 [8, 4096, 512], P('expert'), may hold values from -0.09375 to 0.09375
- tower_in: bfloat16 [512, 2048], replicated, may hold values from -0.25 to 0.25
- tower_out: float32 [8, 256], replicated, may hold values from -0.375 to 0.375
- labels: float32 [16384, 8], P(('table', 'expert')), may hold values from 0 to 1
Outputs:
- grad_rows: float32 [8192, 128], P(('table', 'expert'))
- grad_tower_in: float32 [512, 2048], replicated
- grad_tower_out: float32 [8, 256], replicated
The draws below stay inside these ranges and needn't reach their ends.
Inputs may be any that keep to these rules, and one draw needn't show every extreme that they name: `route_ids`: among the rows of one device, no expert is named by more than 48 rows, a bound that some block reaches; a row names two different experts.
All inputs are finite; a program needn't handle non-finite values.
Results may differ from the reference program's by a relative error of at most 0.015.
Values may be sent and summed in bfloat16 or wider, within the bound.
A program may use at most 128 MiB of HBM per device.

```python
import math
import jax
import jax.numpy as jnp
import numpy as np
from jax import lax

DIM = 128
TABLES = 8
BAG = 4
HID = 4096
EOUT = 512
TASKS = 8
TOWER = 256
B_DEV = 128
F = 1024
EXPERTS = 8
CAP = 48
BATCH = 16384
ROWS = 8192


def place_ends(entries, rng, least, top_value):
    spot = [jax.random.randint(jax.random.fold_in(rng, axis), (), 0, length) for axis, length in enumerate(entries.shape)]
    main_axis = entries.shape.index(max(entries.shape))
    beside = spot[:main_axis] + [(spot[main_axis] + 1) % entries.shape[main_axis]] + spot[main_axis + 1:]
    return entries.at[tuple(spot)].set(least).at[tuple(beside)].set(top_value)


def block_levels(key, extent, cuts, smallest, top_value):
    def one(dim, parts):
        heights = jax.random.uniform(jax.random.fold_in(jax.random.fold_in(key, 6), dim), (parts,), jnp.float32, smallest / len(cuts), top_value / len(cuts))
        return jnp.repeat(jnp.exp(heights), extent[dim] // parts).reshape((-1,) + (1,) * (len(extent) - dim - 1))

    level = one(*cuts[0])
    for cut in cuts[1:]:
        level = level * one(*cut)
    return level


def rank_table(amount, lean):
    loads = [(1 << 20) // math.isqrt(rank ** lean) + 1 for rank in range(1, amount + 1)]
    width = 1 + sum(loads) // (1 << 30)
    return np.cumsum(np.array([max(1, weight // width) for weight in loads]))


def ranked(key, shape, count, slope):
    table = rank_table(count, slope)
    lot = jax.random.randint(jax.random.fold_in(key, 1), shape, 0, int(table[count - 1]))
    standing = jnp.searchsorted(jnp.asarray(table, jnp.int32), lot, side="right")
    return jax.random.permutation(jax.random.fold_in(key, 2), count)[standing].astype(jnp.int32)


def routed_block(rng, own, number, rows, count, top, reach, slope):
    sequence = jax.random.permutation(rng, count)
    packed, ordinary = shares(count, rows * top, reach, slope, True), shares(count, rows * top, reach, slope, False)
    places = jnp.arange(count)

    def named(tallies, offset_by):
        used = int((tallies > 0).sum())
        fixed = max(1, used // 4)
        passed = fixed + (places - fixed + offset_by * (used - fixed)) % max(1, count - fixed)
        return jnp.zeros((count,), jnp.int32).at[sequence[jnp.where(places < fixed, places, passed)]].set(jnp.asarray(tallies, jnp.int32))

    tallies = jnp.where(number % 4 == 0, named(packed, number // 4), named(ordinary, number - number // 4 - 1))
    mixed = jax.random.permutation(jax.random.fold_in(own, 3), count)
    giver, sink = mixed[0:count // 2 * 2:2], mixed[1:count // 2 * 2:2]
    margin = jnp.minimum(tallies[giver] - 1, reach - tallies[sink]) // 2
    margin = jnp.where((giver == sequence[0]) | (sink == sequence[0]) | (tallies[sink] == 0), 0, jnp.maximum(margin, 0))
    passed = jax.random.randint(jax.random.fold_in(own, 4), (count // 2,), 0, 1 << 20) % (margin + 1)
    tallies = tallies.at[giver].add(-passed).at[sink].add(passed)
    items = jnp.searchsorted(jnp.cumsum(tallies), jnp.arange(rows * top), side="right").astype(jnp.int32)
    grid = items.reshape(top, rows).T
    grid = grid[jax.random.permutation(jax.random.fold_in(own, 1), rows)]
    offset_by = jax.random.randint(jax.random.fold_in(own, 2), (rows, 1), 0, top)
    return jnp.take_along_axis(grid, (jnp.arange(top)[None, :] + offset_by) % top, axis=1)


def shares(amount, total, most, skew, full):
    loads = [(1 << 20) // math.isqrt(grade ** skew) + 1 for grade in range(1, amount + 1)]
    largest = most if full else min(most, max(-(-total // amount), total * loads[0] // sum(loads)))
    least = 1 if total - largest >= amount - 1 else 0
    counts, spare = [largest] + [least] * (amount - 1), total - largest - least * (amount - 1)
    while spare > 0:
        candidates = [i for i in range(1, amount) if counts[i] < largest] or [i for i in range(1, amount) if counts[i] < most]
        mass, budget = sum([loads[i] for i in candidates]), spare
        for i in candidates:
            addition = min(most - counts[i], max(1, budget * loads[i] // mass), spare)
            counts[i] = counts[i] + addition
            spare = spare - addition
    return np.array(counts)


def bell_draw(key, extent, scale, limit, pieces=(), kind=jnp.bfloat16):
    drawn = jax.random.normal(key, extent, jnp.float32) * scale
    if len(pieces) > 0:
        drawn = block_levels(key, extent, pieces, -0.22, 0.18) * drawn
    return jnp.clip(drawn, min=-limit, max=limit).astype(kind)


def setup_inputs(seed: int = 0) -> dict:
    arg_keys = jax.random.split(jax.random.key(seed), 10)
    emb_rows = bell_draw(arg_keys[0], (ROWS, DIM), 0.5, 3.0, ((0, 16),))
    row_ids = place_ends(ranked(arg_keys[1], (BATCH, TABLES, BAG), ROWS, 2), jax.random.fold_in(arg_keys[1], 3), 0, ROWS - 1).astype(jnp.int32)
    route_ids_keys = jax.random.split(jax.random.fold_in(arg_keys[2], 1), BATCH // B_DEV)
    route_ids_turns = jax.random.permutation(jax.random.fold_in(arg_keys[2], 3), BATCH // B_DEV)
    route_ids = jax.vmap(lambda own, number: routed_block(jax.random.fold_in(arg_keys[2], 2), own, number, B_DEV, EXPERTS, 2, CAP, 2))(route_ids_keys, route_ids_turns).reshape((BATCH, 2))
    route_gates = jnp.clip(0.1 + 0.9 * jax.random.uniform(arg_keys[3], (BATCH, 2), jnp.float32) ** block_levels(arg_keys[3], (BATCH, 2), ((0, 128),), -0.2, 0.2), 0.1, 1.0)
    w_in = bell_draw(arg_keys[4], (EXPERTS, F, HID), F ** -0.5, 0.1875, ((0, 8),))
    w_out = bell_draw(arg_keys[5], (EXPERTS, HID, EOUT), HID ** -0.5, 0.09375, ((0, 8),))
    tower_in = bell_draw(arg_keys[6], (EOUT, TASKS * TOWER), EOUT ** -0.5, 0.25)
    tower_out = bell_draw(arg_keys[7], (TASKS, TOWER), TOWER ** -0.5, 0.375, (), jnp.float32)
    labels = jnp.clip(1.0 * jax.random.uniform(arg_keys[8], (BATCH, TASKS), jnp.float32) ** block_levels(arg_keys[8], (BATCH, TASKS), ((0, 128),), -0.2, 0.2), 0.0, 1.0)
    return dict(emb_rows=emb_rows, row_ids=row_ids, route_ids=route_ids, route_gates=route_gates, w_in=w_in, w_out=w_out, tower_in=tower_in, tower_out=tower_out, labels=labels)


def silu_grad(pre):
    sig = jax.nn.sigmoid(pre)
    return sig * (1.0 + pre * (1.0 - sig))

def reference(emb_rows, row_ids, route_ids, route_gates, w_in, w_out, tower_in, tower_out, labels):
    count = BATCH // B_DEV
    picked = emb_rows[row_ids].astype(jnp.float32)
    pooled = lax.optimization_barrier(jnp.sum(picked, axis=2))
    tokens = pooled.reshape(BATCH, F).astype(jnp.bfloat16)
    blocks = route_ids.reshape(count, B_DEV * 2)
    onehot = (blocks[:, :, None] == jnp.arange(EXPERTS, dtype=jnp.int32)[None, None, :]).astype(jnp.int32)
    position = lax.optimization_barrier(jnp.sum((jnp.cumsum(onehot, axis=1) - onehot) * onehot, axis=2)).astype(jnp.int32)
    source = jnp.broadcast_to(jnp.arange(count, dtype=jnp.int32)[:, None], blocks.shape)
    expanded = jnp.broadcast_to(tokens[:, None, :], (BATCH, 2, F)).reshape(count, B_DEV * 2, F)
    slots = jnp.zeros((EXPERTS, count, CAP, F), jnp.bfloat16).at[blocks, source, position].set(expanded)

    def forward(inputs):
        rows, first, second = inputs
        pre = jnp.dot(rows.reshape(-1, F), first, preferred_element_type=jnp.float32)
        hidden = jax.nn.silu(pre).astype(jnp.bfloat16)
        made = jnp.dot(hidden, second, preferred_element_type=jnp.float32).astype(jnp.bfloat16)
        return made.reshape(count, CAP, EOUT)
    produced = lax.map(forward, (slots, w_in, w_out))
    expert_out = produced[blocks, source, position].reshape(BATCH, 2, EOUT).astype(jnp.float32)
    combined = lax.optimization_barrier(jnp.sum(route_gates[:, :, None] * expert_out, axis=1)).astype(jnp.bfloat16)
    tower_pre = jnp.dot(combined, tower_in, preferred_element_type=jnp.float32)
    units = jax.nn.silu(tower_pre).reshape(BATCH, TASKS, TOWER)
    logits = lax.optimization_barrier(jnp.sum(units * tower_out[None, :, :], axis=2))
    dlogits = (jax.nn.sigmoid(logits) - labels) / TASKS
    grad_tower_out = jnp.einsum('bk,bki->ki', dlogits, units)
    dunits = dlogits[:, :, None] * tower_out[None, :, :]
    dtower = (dunits.reshape(BATCH, TASKS * TOWER) * silu_grad(tower_pre)).astype(jnp.bfloat16)
    grad_tower_in = jnp.einsum('bd,bh->dh', combined, dtower, preferred_element_type=jnp.float32)
    dcombined = jnp.einsum('bh,dh->bd', dtower, tower_in, preferred_element_type=jnp.float32)
    dentries = (route_gates[:, :, None] * dcombined[:, None, :]).astype(jnp.bfloat16)
    dentries = dentries.reshape(count, B_DEV * 2, EOUT)
    dslots = jnp.zeros((EXPERTS, count, CAP, EOUT), jnp.bfloat16).at[blocks, source, position].set(dentries)

    def backward(inputs):
        rows, grads, first, second = inputs
        pre = jnp.dot(rows.reshape(-1, F), first, preferred_element_type=jnp.float32)
        dhidden = jnp.einsum('ce,he->ch', grads.reshape(-1, EOUT), second, preferred_element_type=jnp.float32)
        dpre = (dhidden * silu_grad(pre)).astype(jnp.bfloat16)
        back = jnp.einsum('ch,fh->cf', dpre, first, preferred_element_type=jnp.float32).astype(jnp.bfloat16)
        return back.reshape(count, CAP, F)
    dtokens = lax.map(backward, (slots, dslots, w_in, w_out))
    dentry = dtokens[blocks, source, position].reshape(BATCH, 2, F).astype(jnp.float32)
    dpooled = lax.optimization_barrier(jnp.sum(dentry, axis=1)).astype(jnp.bfloat16).reshape(BATCH, TABLES, DIM)
    spread = jnp.broadcast_to(dpooled[:, :, None, :].astype(jnp.float32), (BATCH, TABLES, BAG, DIM))
    grad_rows = jax.ops.segment_sum(spread.reshape(-1, DIM), row_ids.reshape(-1), num_segments=ROWS)
    return (grad_rows, grad_tower_in, grad_tower_out)
```

```python
import functools

import jax
import jax.numpy as jnp
from jax import lax
from jax.experimental import pallas as pl
from jax.experimental.pallas import tpu as pltpu
from jax.sharding import PartitionSpec as P

MESH = pl.DeviceIdType.MESH
F32 = jnp.float32
BF16 = jnp.bfloat16
LANES = 128
HALVES = 2
CHUNK = 256
TILE = 512


def dot(a, b):
    return lax.dot_general(a, b, (((1,), (0,)), ((), ())), preferred_element_type=F32)


def dot_nt(a, b):
    return lax.dot_general(a, b, (((1,), (1,)), ((), ())), preferred_element_type=F32)


def silu_grad(pre, sig):
    return sig * (1.0 + pre * (1.0 - sig))


def kernel(
    n_table,
    n_expert,
    ids_ref,
    emb_ref,
    route_ref,
    gate_ref,
    labels_ref,
    tout_ref,
    w_in_hbm,
    w_out_hbm,
    tin_hbm,
    grows_ref,
    gin_hbm,
    gtout_ref,
    w_in,
    w_out,
    tin,
    ids,
    counts,
    rows,
    part_out,
    part_in,
    tokens,
    place,
    place_sum,
    place_t,
    place_both_t,
    outbox,
    inbox,
    acc,
    slope,
    made,
    returned,
    comb,
    dtow,
    dtow_own,
    comb_t,
    tower_out_box,
    tower_in_box,
    tower_x_out,
    tower_x_in,
    gin,
    gto_box,
    gto_mid,
    gto_last,
    dout,
    din,
    dpre,
    drows,
    dback,
    dpooled_t,
    gsend,
    grecv,
    gx_out,
    gx_in,
    wsem,
    loc_sem,
    sib_s,
    sib_r,
    emb_s,
    emb_r,
    box_s,
    box_r,
    back_s,
    back_r,
    dbox_s,
    dbox_r,
    dback_s,
    dback_r,
    tw_s,
    tw_r,
    twx_s,
    twx_r,
    twg_s,
    twg_r,
    twa_s,
    twa_r,
    gto_s,
    gto_r,
    gto2_s,
    gto2_r,
    g_s,
    g_r,
    gx_s,
    gx_r,
):
    t = lax.axis_index("table")
    e = lax.axis_index("expert")
    n_x = n_expert // 2
    x = e // 2
    core = e % 2
    sib = 1 - core
    batch = ids_ref.shape[0]
    lookups = ids_ref.shape[1]
    n_feat = tokens.shape[1] // LANES
    bag = lookups // n_feat
    cap = inbox.shape[1]
    slots = n_expert * cap
    width = tokens.shape[1]
    hid = w_in.shape[1]
    eout = w_out.shape[1]
    tasks, tw = tout_ref.shape
    per = emb_ref.shape[2]
    span = n_x * per
    cols = n_table * span
    n_chunks = width // CHUNK
    rel_per = n_expert // HALVES

    def rel_expert(i):
        return lax.rem(x + i // 2, n_x) * 2 + lax.rem(core + lax.rem(i, 2), 2)

    def rel_back(i):
        return lax.rem(n_x - i // 2, n_x) * 2 + lax.rem(i, 2)

    def remote(src, dst, ssem, rsem, to_t, to_e):
        return pltpu.make_async_remote_copy(
            src_ref=src, dst_ref=dst, send_sem=ssem, recv_sem=rsem,
            device_id=(to_t, to_e), device_id_type=MESH,
        )

    def to_sibling(src, dst, k):
        return remote(src, dst, sib_s.at[k], sib_r.at[k], t, x * 2 + sib)

    def fan_table(src, dst, ssem, rsem):
        def copy(i, at):
            peer = lax.rem(t + i, n_table)
            return remote(src(peer), dst(at(peer)), ssem.at[i], rsem.at[at(peer)], peer, e)

        def start():
            @pl.loop(1, n_table)
            def _(i):
                copy(i, lambda peer: t).start()

        def wait_recv():
            @pl.loop(1, n_table)
            def _(i):
                copy(i, lambda peer: peer).wait_recv()

        def wait_send():
            @pl.loop(1, n_table)
            def _(i):
                copy(i, lambda peer: t).wait_send()

        return start, wait_recv, wait_send

    def fan_x(src, dst, ssem, rsem):
        def copy(i, at):
            peer = lax.rem(x + i, n_x)
            return remote(src(peer), dst(at(peer)), ssem.at[i], rsem.at[at(peer)], t, peer * 2 + core)

        def start():
            @pl.loop(1, n_x)
            def _(i):
                copy(i, lambda peer: x).start()

        def wait_recv():
            @pl.loop(1, n_x)
            def _(i):
                copy(i, lambda peer: peer).wait_recv()

        def wait_send():
            @pl.loop(1, n_x)
            def _(i):
                copy(i, lambda peer: x).wait_send()

        return start, wait_recv, wait_send

    w_in_copy = pltpu.make_async_copy(w_in_hbm, w_in, wsem.at[0])
    w_out_copy = pltpu.make_async_copy(w_out_hbm, w_out, wsem.at[1])
    tin_copy = pltpu.make_async_copy(tin_hbm, tin, wsem.at[2])
    w_in_copy.start()
    w_out_copy.start()
    tin_copy.start()

    barrier = pltpu.get_barrier_semaphore()

    @pl.loop(1, n_table)
    def _(i):
        pl.semaphore_signal(barrier, inc=1, device_id=(lax.rem(t + i, n_table), e), device_id_type=MESH)

    @pl.loop(1, n_expert)
    def _(i):
        pl.semaphore_signal(barrier, inc=1, device_id=(t, lax.rem(e + i, n_expert)), device_id_type=MESH)

    ids[0] = jnp.zeros((batch, LANES), jnp.int32)
    ids[0, :, 0:lookups] = ids_ref[...]
    rows[t] = emb_ref[:, core].reshape(span, LANES)
    pl.semaphore_wait(barrier, n_table + n_expert - 2)

    ids_copy = to_sibling(ids.at[0], ids.at[1], 0)
    ids_copy.start()
    emb_start, emb_recv, emb_send = fan_table(lambda p: rows.at[t], lambda s: rows.at[s], emb_s, emb_r)
    emb_start()

    lane = lax.broadcasted_iota(jnp.int32, (batch, LANES), 1)
    slot_lane = lax.broadcasted_iota(jnp.int32, (batch, slots), 1)
    r0, r1 = route_ref[:, 0:1], route_ref[:, 1:2]
    named0, named1 = lane == r0, lane == r1
    named = jnp.where(named0 | named1, 1.0, 0.0).astype(BF16)
    earlier = jnp.where(
        lax.broadcasted_iota(jnp.int32, (batch, batch), 1) < lax.broadcasted_iota(jnp.int32, (batch, batch), 0),
        1.0, 0.0,
    ).astype(BF16)
    before = dot(earlier, named)
    placed = []
    for j, (r, hit) in enumerate(((r0, named0), (r1, named1))):
        pos = jnp.sum(jnp.where(hit, before, 0.0), axis=1, keepdims=True).astype(jnp.int32)
        placed.append(jnp.where(slot_lane == r * cap + pos, 1.0, 0.0))
        place[j] = placed[j].astype(BF16)
        place_both_t[:, j * batch : (j + 1) * batch] = placed[j].T.astype(BF16)
    both = placed[0] + placed[1]
    place_sum[...] = both.astype(BF16)
    place_t[...] = both.T.astype(BF16)

    @pl.loop(0, 2)
    def _(s):
        @pl.when(s == 1)
        def _():
            ids_copy.wait_recv()

        own = ids[s]
        near = (own // (2 * per)) * per + lax.rem(own, per)
        code = jnp.where(lax.rem(own // per, 2) == core, near, -1)
        for f in range(n_feat):
            high = []
            for k in range(bag):
                c = f * bag + k
                gap = code[:, c : c + 1] - lane
                high.append(jnp.where(jnp.bitwise_and(gap, LANES - 1) == 0, gap >> 7, -1).astype(BF16))

            @pl.loop(0, cols // LANES, unroll=4)
            def _(h):
                mark = h.astype(F32).astype(BF16)
                total = jnp.where(high[0] == mark, 1.0, 0.0).astype(BF16)
                for k in range(1, bag):
                    total += jnp.where(high[k] == mark, 1.0, 0.0).astype(BF16)
                counts[s, f * batch : (f + 1) * batch, pl.ds(pl.multiple_of(h * LANES, LANES), LANES)] = total

    emb_recv()

    def partial(s, c):
        block = counts[s, pl.ds(pl.multiple_of(c * CHUNK, CHUNK), CHUNK), :]
        return dot(block, rows[...].reshape(cols, LANES))

    def part_copy(c):
        return to_sibling(part_out.at[c], part_in.at[c], 1 + c)

    @pl.loop(0, n_chunks)
    def _(c):
        part_out[c] = partial(1, c)
        part_copy(c).start()

    per_chunk = CHUNK // LANES

    @pl.loop(0, n_chunks)
    def _(c):
        mine = partial(0, c)
        part_copy(c).wait_recv()
        pooled = (mine + part_in[c]).astype(BF16)
        for f in range(per_chunk):
            tokens[:, pl.ds(pl.multiple_of(c * CHUNK + f * LANES, LANES), LANES)] = pooled[f * batch : (f + 1) * batch]

    outbox[...] = dot(place_t[...], tokens[...]).astype(BF16).reshape(n_expert, cap, width)

    def box_copy(i, sending):
        peer = rel_expert(i)
        at = rel_back(i) if sending else i
        return remote(outbox.at[peer], inbox.at[at], box_s.at[i], box_r.at[at], t, peer)

    @pl.loop(1, n_expert)
    def _(i):
        box_copy(i, True).start()

    inbox[0] = outbox[e]

    w_in_copy.wait()
    w_out_copy.wait()

    def back_copy(i, sending):
        peer = rel_expert(i)
        at = e if sending else peer
        return remote(made.at[i], returned.at[at], back_s.at[i], back_r.at[at], t, peer)

    m_rows = rel_per * cap

    @pl.loop(0, HALVES)
    def _(half):
        @pl.loop(0, rel_per)
        def _(k):
            i = half * rel_per + k

            @pl.when(i > 0)
            def _():
                box_copy(i, False).wait_recv()

        acc[...] = jnp.zeros_like(acc)

        @pl.loop(0, hid // TILE)
        def _(n):
            at = pl.ds(pl.multiple_of(n * TILE, TILE), TILE)
            block = inbox[pl.ds(half * rel_per, rel_per)].reshape(m_rows, width)
            pre = dot(block, w_in[:, at])
            sig = jax.nn.sigmoid(pre)
            slope[half, :, at] = silu_grad(pre, sig).astype(BF16)
            acc[...] += dot((pre * sig).astype(BF16), w_out[at, :])

        made[pl.ds(half * rel_per, rel_per)] = acc[...].astype(BF16).reshape(rel_per, cap, eout)

        @pl.loop(0, rel_per)
        def _(k):
            i = half * rel_per + k

            @pl.when(i > 0)
            def _():
                back_copy(i, True).start()

    returned[e] = made[0]
    tin_copy.wait()

    @pl.loop(1, n_expert)
    def _(i):
        back_copy(i, False).wait_recv()

    gate0, gate1 = gate_ref[:, 0:1], gate_ref[:, 1:2]
    answers = returned[...].reshape(slots, eout)
    combined = (gate0 * dot(place[0], answers) + gate1 * dot(place[1], answers)).astype(BF16)
    comb[0] = combined
    dcomb = jnp.zeros((batch, eout), F32)
    per_half = tasks // 2
    for k in range(tasks):
        pre = dot(combined, tin[:, k * tw : (k + 1) * tw])
        sig = jax.nn.sigmoid(pre)
        units = pre * sig
        out_row = tout_ref[k : k + 1, :]
        logit = jnp.sum(units * out_row, axis=1, keepdims=True)
        dlogit = (jax.nn.sigmoid(logit) - labels_ref[:, k : k + 1]) / tasks
        gto_box[t, k : k + 1, :] = jnp.sum(dlogit * units, axis=0, keepdims=True)
        grad = (dlogit * out_row * silu_grad(pre, sig)).astype(BF16)
        dtow[k // per_half, :, (k % per_half) * tw : (k % per_half + 1) * tw] = grad
        dcomb += dot_nt(grad, tin[:, k * tw : (k + 1) * tw])
    dent = jnp.concatenate([(gate0 * dcomb).astype(BF16), (gate1 * dcomb).astype(BF16)], axis=0)
    dout[...] = dot(place_both_t[...], dent).astype(BF16).reshape(n_expert, cap, eout)

    def dbox_copy(i, sending):
        peer = rel_expert(i)
        at = rel_back(i) if sending else i
        return remote(dout.at[peer], din.at[at], dbox_s.at[i], dbox_r.at[at], t, peer)

    @pl.loop(1, n_expert)
    def _(i):
        dbox_copy(i, True).start()

    din[0] = dout[e]

    k_comb = 1 + n_chunks
    comb_copy = to_sibling(comb.at[0], comb.at[1], k_comb)
    dtow_copy = to_sibling(dtow.at[sib], dtow_own.at[1], k_comb + 1)
    comb_copy.start()
    dtow_copy.start()
    gto_start, gto_recv, gto_send = fan_table(lambda p: gto_box.at[t], lambda s: gto_box.at[s], gto_s, gto_r)
    gto_start()
    dtow_own[0] = dtow[core]
    comb_copy.wait_recv()
    dtow_copy.wait_recv()
    comb_t[:, 0:batch] = comb[0].astype(F32).T.astype(BF16)
    comb_t[:, batch : 2 * batch] = comb[1].astype(F32).T.astype(BF16)
    t_rows = eout // n_table
    t_cols = tasks * tw // 2
    x_cols = t_cols // n_x
    group = LANES // t_rows
    sides = dtow_own[...].reshape(2 * batch, t_cols)

    @pl.loop(0, eout // LANES)
    def _(i):
        block = dot(comb_t[pl.ds(pl.multiple_of(i * LANES, LANES), LANES), :], dtow_own[...].reshape(2 * batch, t_cols))
        tower_out_box[pl.ds(i * group, group)] = block.astype(BF16).reshape(group, t_rows, t_cols)

    tw_start, tw_recv, tw_send = fan_table(
        lambda p: tower_out_box.at[p], lambda s: tower_in_box.at[s], tw_s, tw_r
    )
    tw_start()
    tower_in_box[t] = tower_out_box[t]

    @pl.loop(0, HALVES)
    def _(half):
        @pl.loop(0, rel_per)
        def _(k):
            i = half * rel_per + k

            @pl.when(i > 0)
            def _():
                dbox_copy(i, False).wait_recv()

        @pl.loop(0, hid // TILE)
        def _(n):
            at = pl.ds(pl.multiple_of(n * TILE, TILE), TILE)
            block = din[pl.ds(half * rel_per, rel_per)].reshape(m_rows, eout)
            dhid = dot_nt(block, w_out[at, :])
            dpre[half, :, at] = (dhid * slope[half, :, at].astype(F32)).astype(BF16)

    def dback_copy(c, i, sending):
        peer = rel_expert(i)
        at = e if sending else peer
        return remote(drows.at[c, i], dback.at[c, at], dback_s.at[c, i], dback_r.at[c, at], t, peer)

    @pl.loop(0, n_chunks)
    def _(c):
        at = pl.ds(pl.multiple_of(c * CHUNK, CHUNK), CHUNK)

        @pl.loop(0, HALVES)
        def _(half):
            block = dot_nt(dpre[half], w_in[at, :])
            drows[c, pl.ds(half * rel_per, rel_per)] = block.astype(BF16).reshape(rel_per, cap, CHUNK)

            @pl.loop(0, rel_per)
            def _(k):
                i = half * rel_per + k

                @pl.when(i > 0)
                def _():
                    dback_copy(c, i, True).start()

        dback[c, e] = drows[c, 0]

    tw_recv()
    total = tower_in_box[0].astype(F32)
    for s in range(1, n_table):
        total += tower_in_box[s].astype(F32)
    for k in range(n_x):
        tower_x_out[k] = total[:, k * x_cols : (k + 1) * x_cols].astype(BF16)
    twx_start, twx_recv, twx_send = fan_x(lambda p: tower_x_out.at[p], lambda s: tower_x_in.at[s], twx_s, twx_r)
    twx_start()
    tower_x_in[x] = tower_x_out[x]
    gto_recv()
    gsum = gto_box[0]
    for s in range(1, n_table):
        gsum += gto_box[s]
    gto_last[e] = gsum
    gto_mid[...] = gsum

    def gto2_copy(i, sending):
        peer = lax.rem(e + i, n_expert)
        at = e if sending else peer
        return remote(gto_mid, gto_last.at[at], gto2_s.at[i], gto2_r.at[at], t, peer)

    @pl.loop(1, n_expert)
    def _(i):
        gto2_copy(i, True).start()

    twx_recv()
    total = tower_x_in[0].astype(F32)
    for s in range(1, n_x):
        total += tower_x_in[s].astype(F32)

    def gin_rows(s):
        return pl.ds(pl.multiple_of(s * t_rows, t_rows), t_rows)

    def gin_block(s):
        return gin.at[core, gin_rows(t), pl.ds(pl.multiple_of(s * x_cols, x_cols), x_cols)]

    gin[core, gin_rows(t), pl.ds(pl.multiple_of(x * x_cols, x_cols), x_cols)] = total.astype(BF16)
    twg_start, twg_recv, twg_send = fan_x(lambda p: gin_block(x), gin_block, twg_s, twg_r)
    twg_start()
    twg_recv()
    twa_start, twa_recv, twa_send = fan_table(
        lambda p: gin.at[core, gin_rows(t)], lambda s: gin.at[core, gin_rows(s)], twa_s, twa_r
    )
    twa_start()

    def dpool_copy(c):
        k = k_comb + 2 + c
        at = pl.multiple_of(c * CHUNK, CHUNK)
        return to_sibling(
            dpooled_t.at[:, pl.ds(at, CHUNK)], dpooled_t.at[:, pl.ds(width + at, CHUNK)], k
        )

    @pl.loop(0, n_chunks)
    def _(c):
        @pl.loop(1, n_expert)
        def _(i):
            dback_copy(c, i, False).wait_recv()

        got = dot(place_sum[...], dback[c].reshape(slots, CHUNK)).astype(BF16).astype(F32)
        for f in range(per_chunk):
            at = pl.multiple_of(c * CHUNK + f * LANES, LANES)
            dpooled_t[:, pl.ds(at, LANES)] = got[:, f * LANES : (f + 1) * LANES].T.astype(BF16)
        dpool_copy(c).start()

    @pl.loop(0, n_chunks)
    def _(c):
        dpool_copy(c).wait_recv()

    def shard_grads(p):
        block = counts[:, :, pl.ds(pl.multiple_of(p * span, span), span)].reshape(2 * width, span)
        return dot(dpooled_t[...], block).astype(BF16)

    def g_copy(i, sending):
        peer = lax.rem(t + i, n_table)
        at = t if sending else peer
        return remote(gsend.at[peer], grecv.at[at], g_s.at[i], g_r.at[at], peer, e)

    @pl.loop(1, n_table)
    def _(i):
        peer = lax.rem(t + i, n_table)
        gsend[peer] = shard_grads(peer)
        g_copy(i, True).start()

    grecv[t] = shard_grads(t)

    twa_recv()
    gin_copy = to_sibling(gin.at[core], gin.at[core], k_comb + 2 + n_chunks)
    gin_copy.start()

    @pl.loop(1, n_expert)
    def _(i):
        gto2_copy(i, False).wait_recv()

    gsum = gto_last[0]
    for s in range(1, n_expert):
        gsum += gto_last[s]
    gtout_ref[...] = gsum

    to_sibling(gin.at[sib], gin.at[sib], k_comb + 2 + n_chunks).wait_recv()
    gin_outs = [
        pltpu.make_async_copy(gin.at[h], gin_hbm.at[:, pl.ds(h * t_cols, t_cols)], loc_sem.at[h]) for h in range(2)
    ]
    for copy in gin_outs:
        copy.start()

    @pl.loop(1, n_table)
    def _(i):
        g_copy(i, False).wait_recv()

    total = grecv[0].astype(F32)
    for s in range(1, n_table):
        total += grecv[s].astype(F32)
    gx_out[...] = total.T.astype(BF16).reshape(n_x, per, LANES)
    gx_start, gx_recv, gx_send = fan_x(lambda p: gx_out.at[p], lambda s: gx_in.at[s], gx_s, gx_r)
    gx_start()
    gx_in[x] = gx_out[x]
    gx_recv()
    total = gx_in[0].astype(F32)
    for s in range(1, n_x):
        total += gx_in[s].astype(F32)
    grows_ref[...] = total

    ids_copy.wait_send()
    emb_send()
    comb_copy.wait_send()
    dtow_copy.wait_send()
    gto_send()
    tw_send()
    twx_send()
    twg_send()
    twa_send()
    gin_copy.wait_send()
    gx_send()

    @pl.loop(0, n_chunks)
    def _(c):
        part_copy(c).wait_send()
        dpool_copy(c).wait_send()

        @pl.loop(1, n_expert)
        def _(i):
            dback_copy(c, i, True).wait_send()

    @pl.loop(1, n_expert)
    def _(i):
        box_copy(i, True).wait_send()
        back_copy(i, True).wait_send()
        dbox_copy(i, True).wait_send()
        gto2_copy(i, True).wait_send()

    @pl.loop(1, n_table)
    def _(i):
        g_copy(i, True).wait_send()

    for copy in gin_outs:
        copy.wait()


def per_device(emb_rows, row_ids, route_ids, route_gates, w_in, w_out, tower_in, tower_out, labels):
    n_table = lax.axis_size("table")
    n_expert = lax.axis_size("expert")
    n_x = n_expert // 2
    samples, tables, bag = row_ids.shape
    cap = 3 * samples // n_expert
    row_dev, dim = emb_rows.shape
    width = tables * dim
    hid, eout = w_out.shape[1:]
    tasks, tw = tower_out.shape
    per = row_dev // n_expert
    span = n_x * per
    cols = n_table * span
    slots = n_expert * cap
    n_chunks = width // CHUNK
    m_rows = slots // HALVES
    t_rows = eout // n_table
    t_cols = tasks * tw // 2
    x_cols = t_cols // n_x
    n_sib = 1 + n_chunks + 2 + n_chunks + 1
    vmem = pl.BlockSpec(memory_space=pltpu.VMEM)
    hbm = pl.BlockSpec(memory_space=pl.ANY)
    dma = pltpu.SemaphoreType.DMA
    scratch = [
        pltpu.VMEM((width, hid), BF16),
        pltpu.VMEM((hid, eout), BF16),
        pltpu.VMEM((eout, tasks * tw), BF16),
        pltpu.VMEM((2, samples, LANES), jnp.int32),
        pltpu.VMEM((2, width, cols), BF16),
        pltpu.VMEM((n_table, span, LANES), BF16),
        pltpu.VMEM((n_chunks, CHUNK, LANES), F32),
        pltpu.VMEM((n_chunks, CHUNK, LANES), F32),
        pltpu.VMEM((samples, width), BF16),
        pltpu.VMEM((2, samples, slots), BF16),
        pltpu.VMEM((samples, slots), BF16),
        pltpu.VMEM((slots, samples), BF16),
        pltpu.VMEM((slots, 2 * samples), BF16),
        pltpu.VMEM((n_expert, cap, width), BF16),
        pltpu.VMEM((n_expert, cap, width), BF16),
        pltpu.VMEM((m_rows, eout), F32),
        pltpu.VMEM((HALVES, m_rows, hid), BF16),
        pltpu.VMEM((n_expert, cap, eout), BF16),
        pltpu.VMEM((n_expert, cap, eout), BF16),
        pltpu.VMEM((2, samples, eout), BF16),
        pltpu.VMEM((2, samples, t_cols), BF16),
        pltpu.VMEM((2, samples, t_cols), BF16),
        pltpu.VMEM((eout, 2 * samples), BF16),
        pltpu.VMEM((n_table, t_rows, t_cols), BF16),
        pltpu.VMEM((n_table, t_rows, t_cols), BF16),
        pltpu.VMEM((n_x, t_rows, x_cols), BF16),
        pltpu.VMEM((n_x, t_rows, x_cols), BF16),
        pltpu.VMEM((2, eout, t_cols), BF16),
        pltpu.VMEM((n_table, tasks, tw), F32),
        pltpu.VMEM((tasks, tw), F32),
        pltpu.VMEM((n_expert, tasks, tw), F32),
        pltpu.VMEM((n_expert, cap, eout), BF16),
        pltpu.VMEM((n_expert, cap, eout), BF16),
        pltpu.VMEM((HALVES, m_rows, hid), BF16),
        pltpu.VMEM((n_chunks, n_expert, cap, CHUNK), BF16),
        pltpu.VMEM((n_chunks, n_expert, cap, CHUNK), BF16),
        pltpu.VMEM((LANES, 2 * width), BF16),
        pltpu.VMEM((n_table, LANES, span), BF16),
        pltpu.VMEM((n_table, LANES, span), BF16),
        pltpu.VMEM((n_x, per, LANES), BF16),
        pltpu.VMEM((n_x, per, LANES), BF16),
        dma((3,)),
        dma((2,)),
        dma((n_sib,)),
        dma((n_sib,)),
        dma((n_table,)),
        dma((n_table,)),
        dma((n_expert,)),
        dma((n_expert,)),
        dma((n_expert,)),
        dma((n_expert,)),
        dma((n_expert,)),
        dma((n_expert,)),
        dma((n_chunks, n_expert)),
        dma((n_chunks, n_expert)),
        dma((n_table,)),
        dma((n_table,)),
        dma((n_x,)),
        dma((n_x,)),
        dma((n_x,)),
        dma((n_x,)),
        dma((n_table,)),
        dma((n_table,)),
        dma((n_table,)),
        dma((n_table,)),
        dma((n_expert,)),
        dma((n_expert,)),
        dma((n_table,)),
        dma((n_table,)),
        dma((n_x,)),
        dma((n_x,)),
    ]
    grows, gin, gtout = pl.pallas_call(
        functools.partial(kernel, n_table, n_expert),
        out_shape=(
            jax.ShapeDtypeStruct((per, dim), F32),
            jax.ShapeDtypeStruct((eout, tasks * tw), BF16),
            jax.ShapeDtypeStruct((tasks, tw), F32),
        ),
        in_specs=[vmem] * 6 + [hbm] * 3,
        out_specs=(vmem, hbm, vmem),
        scratch_shapes=scratch,
        compiler_params=pltpu.CompilerParams(
            collective_id=0, has_side_effects=True, vmem_limit_bytes=VMEM_LIMIT
        ),
    )(
        row_ids.reshape(samples, tables * bag),
        emb_rows.reshape(n_x, 2, per, dim),
        route_ids,
        route_gates,
        labels,
        tower_out,
        w_in[0],
        w_out[0],
        tower_in,
    )
    return grows, gin.astype(F32), gtout


VMEM_LIMIT = 62 * 1024 * 1024


def solution(mesh):
    return jax.shard_map(
        per_device,
        mesh=mesh,
        in_specs=(
            P("table", None),
            P(("table", "expert"), None, None),
            P(("table", "expert"), None),
            P(("table", "expert"), None),
            P("expert", None, None),
            P("expert", None, None),
            P(),
            P(),
            P(("table", "expert"), None),
        ),
        out_specs=(P(("table", "expert"), None), P(), P()),
        check_vma=False,
    )
```

```python
import functools
import math

import jax
import jax.numpy as jnp
from jax import lax
from jax.experimental import pallas as pl
from jax.experimental.pallas import tpu as pltpu
from jax.sharding import PartitionSpec as P

MESH = pl.DeviceIdType.MESH
F32 = jnp.float32
BF16 = jnp.bfloat16
LANES = 128
HALVES = 2
CHUNK = 256
TILE = 512


IDS, EMB_A, EMB_B, COMB, DTOW, GTO_A, GTO_B, GTO_E = range(8)
TOW_A, TOW_B, TOW_X, GIN_X, GIN_B, GIN_A, GIN_S = range(8, 15)
BACK, GRAD_A, GRAD_B, GRAD_X = range(15, 19)
DBOX = 20
PART = 24
DBACK = 28
DPOOL = 32
BOX = 36
N_SEMS = 44


def dot(a, b):
    return lax.dot_general(a, b, (((1,), (0,)), ((), ())), preferred_element_type=F32)


def dot_nt(a, b):
    return lax.dot_general(a, b, (((1,), (1,)), ((), ())), preferred_element_type=F32)


def silu_grad(pre, sig):
    return sig * (1.0 + pre * (1.0 - sig))


def kernel(
    n_table,
    n_expert,
    ids_ref,
    emb_ref,
    route_ref,
    gate_ref,
    labels_ref,
    tout_ref,
    w_in_hbm,
    w_out_hbm,
    tin_hbm,
    grows_ref,
    gin_hbm,
    gtout_ref,
    w_in,
    w_out,
    tin,
    ids,
    narrow,
    counts,
    rows,
    part_out,
    part_in,
    place,
    place_sum,
    place_t,
    place_both_t,
    outbox,
    inbox,
    acc,
    slope,
    made,
    returned,
    comb,
    dtow,
    dtow_own,
    comb_t,
    tower_a_out,
    tower_a_in,
    tower_b_out,
    tower_b_in,
    tower_x_out,
    tower_x_in,
    gin,
    gto_out,
    gto_a,
    gto_b,
    gto_e,
    dout,
    din,
    dpre,
    drows,
    dback,
    dpooled_t,
    grad_acc,
    ga_out,
    ga_in,
    gb_out,
    gb_in,
    gx_out,
    gx_in,
    local_sem,
    ss,
    rs,
):
    t = lax.axis_index("table")
    e = lax.axis_index("expert")
    n_x = n_expert // 2
    side = math.isqrt(n_table)
    x = e // 2
    core = e % 2
    sib = 1 - core
    first = core == 0
    a = jnp.where(first, t // side, t % side)
    b = jnp.where(first, t % side, t // side)
    a_step = jnp.where(first, side, 1)
    b_step = jnp.where(first, 1, side)
    lookups, batch = ids_ref.shape
    n_chunks = outbox.shape[0]
    width = n_chunks * CHUNK
    n_feat = width // LANES
    bag = lookups // n_feat
    cap = inbox.shape[2]
    slots = n_expert * cap
    hid = w_in.shape[1]
    eout = w_out.shape[1]
    tasks, tw = tout_ref.shape
    per = emb_ref.shape[2]
    span = n_x * per
    cols = n_table * span
    rel_per = n_expert // HALVES
    m_rows = rel_per * cap
    per_chunk = CHUNK // LANES

    def rel_expert(i):
        return lax.rem(x + i // 2, n_x) * 2 + lax.rem(core + i % 2, 2)

    def rel_back(i):
        return (n_x - i // 2) % n_x * 2 + i % 2

    rel_order = sorted(range(1, n_expert), key=lambda i: (min(i // 2, n_x - i // 2), -(i // 2)))

    def remote(src, dst, k_send, k_recv, to_t, to_e):
        return pltpu.make_async_remote_copy(
            src_ref=src, dst_ref=dst, send_sem=ss.at[k_send], recv_sem=rs.at[k_recv],
            device_id=(to_t, to_e), device_id_type=MESH,
        )

    def took(ref, sem):
        pltpu.make_async_copy(ref, ref, sem).wait()

    sent = []

    def to_sibling(src, dst, k):
        remote(src, dst, k, k, t, x * 2 + sib).start()
        sent.append((src, k))

    def fan_a(src, dst, k, total):
        for i in range(1, side):
            to = lax.rem(a + i, side)
            remote(src(to), dst, k, k, to * a_step + b * b_step, e).start()
        sent.append((total, k))

    def fan_b(src, dst, k, total):
        for i in range(1, side):
            to = lax.rem(b + i, side)
            remote(src(to), dst, k, k, a * a_step + to * b_step, e).start()
        sent.append((total, k))

    def fan_x(src, dst, k, total):
        for i in range(1, n_x):
            to = lax.rem(x + i, n_x)
            remote(src(to), dst, k, k, t, to * 2 + core).start()
        sent.append((total, k))

    def sum_of(ref, n):
        total = ref[0].astype(F32)
        for i in range(1, n):
            total += ref[i].astype(F32)
        return total

    w_in_copy = pltpu.make_async_copy(w_in_hbm, w_in, local_sem.at[0])
    w_out_copy = pltpu.make_async_copy(w_out_hbm, w_out, local_sem.at[1])
    tin_copy = pltpu.make_async_copy(tin_hbm, tin, local_sem.at[2])

    barrier = pltpu.get_barrier_semaphore()
    for i in range(1, side):
        for to_t in (lax.rem(a + i, side) * a_step + b * b_step, a * a_step + lax.rem(b + i, side) * b_step):
            pl.semaphore_signal(barrier, inc=1, device_id=(to_t, e), device_id_type=MESH)
    for i in range(1, n_expert):
        pl.semaphore_signal(barrier, inc=1, device_id=(t, rel_expert(i)), device_id_type=MESH)

    ids[0] = ids_ref[...]
    rows[a, b] = emb_ref[:, core].reshape(span, LANES)
    pl.semaphore_wait(barrier, 2 * (side - 1) + n_expert - 1)

    fan_a(lambda to: rows.at[a, b], rows.at[a, b], EMB_A, rows.at[0, pl.ds(0, side - 1)])
    to_sibling(ids.at[0], ids.at[1], IDS)
    w_in_copy.start()
    w_out_copy.start()
    tin_copy.start()

    narrow[...] = jnp.zeros_like(narrow)
    narrow[0:2] = route_ref[...].astype(F32)
    narrow[8:10] = gate_ref[...]
    narrow[16 : 16 + tasks] = labels_ref[...]
    columns = narrow[...].T
    lane = lax.broadcasted_iota(jnp.int32, (batch, LANES), 1)
    slot_lane = lax.broadcasted_iota(jnp.int32, (batch, slots), 1)
    r0, r1 = columns[:, 0:1].astype(jnp.int32), columns[:, 1:2].astype(jnp.int32)
    gate0, gate1 = columns[:, 8:9], columns[:, 9:10]
    named0, named1 = lane == r0, lane == r1
    named = jnp.where(named0 | named1, 1.0, 0.0).astype(BF16)
    earlier = jnp.where(
        lax.broadcasted_iota(jnp.int32, (batch, batch), 1) < lax.broadcasted_iota(jnp.int32, (batch, batch), 0),
        1.0, 0.0,
    ).astype(BF16)
    before = dot(earlier, named)
    placed = []
    for j, (r, hit) in enumerate(((r0, named0), (r1, named1))):
        pos = jnp.sum(jnp.where(hit, before, 0.0), axis=1, keepdims=True).astype(jnp.int32)
        placed.append(jnp.where(slot_lane == r * cap + pos, 1.0, 0.0))
        place[j] = placed[j].astype(BF16)
        place_both_t[:, j * batch : (j + 1) * batch] = placed[j].T.astype(BF16)
    both = placed[0] + placed[1]
    place_sum[...] = both.astype(BF16)
    place_t[...] = both.T.astype(BF16)

    def build_counts(s):
        own = ids[s]
        shard = own // (n_x * 2 * per)
        near = lax.rem(own // (2 * per), n_x) * per + lax.rem(own, per)
        at_a = jnp.where(first, shard // side, lax.rem(shard, side))
        at_b = jnp.where(first, lax.rem(shard, side), shard // side)
        code = jnp.where(lax.rem(own // per, 2) == core, (at_a * side + at_b) * span + near, -1)
        flat = jnp.concatenate([code.astype(F32), jnp.zeros((LANES - lookups, batch), F32)], axis=0)
        code = flat.T.astype(jnp.int32)
        for f in range(n_feat):
            words = [jnp.zeros((batch, LANES), jnp.int32) for _ in range(-(-cols // (8 * LANES)))]
            for k in range(bag):
                c = f * bag + k
                gap = code[:, c : c + 1] - lane
                high = gap >> 7
                one = jnp.where(jnp.bitwise_and(gap, LANES - 1) == 0, 1 << (jnp.bitwise_and(high, 7) * 4), 0)
                which = high >> 3
                for w in range(len(words)):
                    words[w] = words[w] + jnp.where(which == w, one, 0)
            for h in range(cols // LANES):
                count = jnp.bitwise_and(words[h // 8] >> (4 * (h % 8)), 15)
                counts[s, f * batch : (f + 1) * batch, h * LANES : (h + 1) * LANES] = count.astype(F32).astype(BF16)

    build_counts(0)
    took(rows.at[0, pl.ds(0, side - 1)], rs.at[EMB_A])
    fan_b(lambda to: rows.at[:, b], rows.at[:, b], EMB_B, rows.at[pl.ds(0, side - 1)])
    took(ids.at[1], rs.at[IDS])
    build_counts(1)
    took(rows.at[pl.ds(0, side - 1)], rs.at[EMB_B])

    def partial(s, c):
        return dot(counts[s, c * CHUNK : (c + 1) * CHUNK, :], rows[...].reshape(cols, LANES))

    def swap_partial(c):
        part_out[c] = partial(1, c)
        to_sibling(part_out.at[c], part_in.at[c], PART + c)

    swap_partial(0)
    for c in range(n_chunks):
        mine = partial(0, c)
        if c + 1 < n_chunks:
            swap_partial(c + 1)
        took(part_in.at[c], rs.at[PART + c])
        pooled = (mine + part_in[c]).astype(BF16)
        tokens = jnp.concatenate([pooled[f * batch : (f + 1) * batch] for f in range(per_chunk)], axis=1)
        outbox[c] = dot(place_t[...], tokens).astype(BF16).reshape(n_expert, cap, CHUNK)
        for i in rel_order:
            at = rel_back(i)
            to = rel_expert(i)
            k = BOX + c * HALVES + at // rel_per
            remote(outbox.at[c, to], inbox.at[c, at], BOX + c, k, t, to).start()
        sent.append((outbox.at[c, pl.ds(0, n_expert - 1)], BOX + c))
        inbox[c, 0] = outbox[c, e]

    w_in_copy.wait()
    w_out_copy.wait()

    def half_rels(half):
        return half * rel_per, rel_per

    def arrived(half):
        return pl.ds(max(1, half * rel_per), rel_per - (half == 0))

    for half in range(HALVES):
        for c in range(n_chunks):
            took(inbox.at[c, arrived(half)], rs.at[BOX + c * HALVES + half])
        acc[...] = jnp.zeros_like(acc)
        mine = slice(half * rel_per, (half + 1) * rel_per)

        @pl.loop(0, hid // TILE)
        def _(n):
            at = pl.ds(pl.multiple_of(n * TILE, TILE), TILE)
            block = jnp.concatenate([inbox[c, mine].reshape(m_rows, CHUNK) for c in range(n_chunks)], axis=1)
            pre = dot(block, w_in[:, at])
            sig = jax.nn.sigmoid(pre)
            slope[half, :, at] = silu_grad(pre, sig).astype(BF16)
            acc[...] += dot((pre * sig).astype(BF16), w_out[at, :])

        made[mine] = acc[...].astype(BF16).reshape(rel_per, cap, eout)
        for i in rel_order:
            if i // rel_per == half:
                remote(made.at[i], returned.at[e], BACK, BACK, t, rel_expert(i)).start()

    sent.append((made.at[pl.ds(1, n_expert - 1)], BACK))
    returned[e] = made[0]
    tin_copy.wait()
    took(returned.at[pl.ds(0, n_expert - 1)], rs.at[BACK])

    answers = returned[...].reshape(slots, eout)
    combined = (gate0 * dot(place[0], answers) + gate1 * dot(place[1], answers)).astype(BF16)
    comb[0] = combined
    dcomb = jnp.zeros((batch, eout), F32)
    per_half = tasks // 2
    for k in range(tasks):
        pre = dot(combined, tin[:, k * tw : (k + 1) * tw])
        sig = jax.nn.sigmoid(pre)
        units = pre * sig
        out_row = tout_ref[k : k + 1, :]
        logit = jnp.sum(units * out_row, axis=1, keepdims=True)
        dlogit = (jax.nn.sigmoid(logit) - columns[:, 16 + k : 17 + k]) / tasks
        gto_out[0, k : k + 1, :] = jnp.sum(dlogit * units, axis=0, keepdims=True)
        grad = (dlogit * out_row * silu_grad(pre, sig)).astype(BF16)
        dtow[k // per_half, :, (k % per_half) * tw : (k % per_half + 1) * tw] = grad
        dcomb += dot_nt(grad, tin[:, k * tw : (k + 1) * tw])
    dent = jnp.concatenate([(gate0 * dcomb).astype(BF16), (gate1 * dcomb).astype(BF16)], axis=0)
    dout[...] = dot(place_both_t[...], dent).astype(BF16).reshape(n_expert, cap, eout)
    for i in rel_order:
        at = rel_back(i)
        to = rel_expert(i)
        remote(dout.at[to], din.at[at], DBOX, DBOX + at // rel_per, t, to).start()
    sent.append((dout.at[pl.ds(0, n_expert - 1)], DBOX))
    din[0] = dout[e]

    to_sibling(comb.at[0], comb.at[1], COMB)
    to_sibling(dtow.at[sib], dtow_own.at[1], DTOW)
    fan_a(lambda to: gto_out.at[0], gto_a.at[a], GTO_A, gto_a.at[pl.ds(0, side - 1)])
    gto_a[a] = gto_out[0]
    dtow_own[0] = dtow[core]
    comb_t[:, 0:batch] = comb[0].astype(F32).T.astype(BF16)
    took(comb.at[1], rs.at[COMB])
    took(dtow_own.at[1], rs.at[DTOW])
    comb_t[:, batch : 2 * batch] = comb[1].astype(F32).T.astype(BF16)
    t_rows = eout // n_table
    t_cols = tasks * tw // 2
    x_cols = t_cols // n_x
    big = side * t_rows

    @pl.loop(0, side)
    def _(i):
        block = dot(comb_t[pl.ds(pl.multiple_of(i * big, big), big), :], dtow_own[...].reshape(2 * batch, t_cols))
        tower_a_out[i] = block.astype(BF16)

    fan_a(lambda to: tower_a_out.at[to], tower_a_in.at[a], TOW_A, tower_a_in.at[pl.ds(0, side - 1)])
    tower_a_in[a] = tower_a_out[a]

    for half in range(HALVES):
        took(din.at[arrived(half)], rs.at[DBOX + half])
        mine = slice(half * rel_per, (half + 1) * rel_per)

        @pl.loop(0, hid // TILE)
        def _(n):
            at = pl.ds(pl.multiple_of(n * TILE, TILE), TILE)
            dhid = dot_nt(din[mine].reshape(m_rows, eout), w_out[at, :])
            dpre[half, :, at] = (dhid * slope[half, :, at].astype(F32)).astype(BF16)

    took(tower_a_in.at[pl.ds(0, side - 1)], rs.at[TOW_A])
    took(gto_a.at[pl.ds(0, side - 1)], rs.at[GTO_A])
    tower_b_out[...] = sum_of(tower_a_in, side).astype(BF16).reshape(side, t_rows, t_cols)
    fan_b(lambda to: tower_b_out.at[to], tower_b_in.at[b], TOW_B, tower_b_in.at[pl.ds(0, side - 1)])
    tower_b_in[b] = tower_b_out[b]
    gto_out[1] = sum_of(gto_a, side)
    fan_b(lambda to: gto_out.at[1], gto_b.at[b], GTO_B, gto_b.at[pl.ds(0, side - 1)])
    gto_b[b] = gto_out[1]

    def token_grads(c):
        for half in range(HALVES):
            block = dot_nt(dpre[half], w_in[c * CHUNK : (c + 1) * CHUNK, :])
            drows[c, half * rel_per : (half + 1) * rel_per] = block.astype(BF16).reshape(rel_per, cap, CHUNK)
        for i in rel_order:
            remote(drows.at[c, i], dback.at[c, e], DBACK + c, DBACK + c, t, rel_expert(i)).start()
        sent.append((drows.at[c, pl.ds(1, n_expert - 1)], DBACK + c))
        dback[c, e] = drows[c, 0]

    def pooled_grads(c):
        took(dback.at[c, pl.ds(0, n_expert - 1)], rs.at[DBACK + c])
        got = dot(place_sum[...], dback[c].reshape(slots, CHUNK)).astype(BF16).astype(F32)
        for f in range(per_chunk):
            dpooled_t[c, 0, :, f * batch : (f + 1) * batch] = got[:, f * LANES : (f + 1) * LANES].T.astype(BF16)
        to_sibling(dpooled_t.at[c, 0], dpooled_t.at[c, 1], DPOOL + c)

    big_cols = side * span

    def row_grads(c, at_a):
        at = pl.ds(pl.multiple_of(at_a * big_cols, big_cols), big_cols)
        total = dot(dpooled_t[c, 0], counts[0, c * CHUNK : (c + 1) * CHUNK, at])
        total += dot(dpooled_t[c, 1], counts[1, c * CHUNK : (c + 1) * CHUNK, at])
        return total if c == 0 else total + grad_acc[at_a]

    def add_chunk(c):
        took(dpooled_t.at[c, 1], rs.at[DPOOL + c])

        @pl.loop(0, side)
        def _(at_a):
            grad_acc[at_a] = row_grads(c, at_a)

    def gin_rows(at, n):
        return pl.ds(pl.multiple_of(at * t_rows, t_rows), n * t_rows)

    my_rows, my_big = gin_rows(a * side + b, 1), gin_rows(a * side, side)
    x_at = pl.ds(pl.multiple_of(x * x_cols, x_cols), x_cols)

    def tower_second():
        took(tower_b_in.at[pl.ds(0, side - 1)], rs.at[TOW_B])
        took(gto_b.at[pl.ds(0, side - 1)], rs.at[GTO_B])
        total = sum_of(tower_b_in, side)
        for k in range(n_x):
            tower_x_out[k] = total[:, k * x_cols : (k + 1) * x_cols].astype(BF16)
        fan_x(lambda to: tower_x_out.at[to], tower_x_in.at[x], TOW_X, tower_x_in.at[pl.ds(0, n_x - 1)])
        tower_x_in[x] = tower_x_out[x]
        gto_out[2] = sum_of(gto_b, side)
        for i in rel_order:
            remote(gto_out.at[2], gto_e.at[e], GTO_E, GTO_E, t, rel_expert(i)).start()
        sent.append((gto_e.at[pl.ds(0, n_expert - 1)], GTO_E))
        gto_e[e] = gto_out[2]

    def tower_x():
        took(tower_x_in.at[pl.ds(0, n_x - 1)], rs.at[TOW_X])
        gin[core, my_rows, x_at] = sum_of(tower_x_in, n_x).astype(BF16)
        block = gin.at[core, my_rows, x_at]
        fan_x(lambda to: block, block, GIN_X, tower_x_in.at[pl.ds(0, n_x - 1)])

    def gather_x():
        took(tower_x_in.at[pl.ds(0, n_x - 1)], rs.at[GIN_X])
        block = gin.at[core, my_rows]
        fan_b(lambda to: block, block, GIN_B, tower_b_in.at[pl.ds(0, side - 1)])

    def gather_b():
        took(tower_b_in.at[pl.ds(0, side - 1)], rs.at[GIN_B])
        block = gin.at[core, my_big]
        fan_a(lambda to: block, block, GIN_A, tower_a_in.at[pl.ds(0, side - 1)])

    beside = {1: tower_second, 3: tower_x}
    for c in range(n_chunks):
        token_grads(c)
        if c in beside:
            beside[c]()
    beside = {1: gather_x, 2: gather_b}
    for c in range(n_chunks):
        pooled_grads(c)
        if c > 0:
            add_chunk(c - 1)
        if c in beside:
            beside[c]()

    last = n_chunks - 1
    took(dpooled_t.at[last, 1], rs.at[DPOOL + last])
    for i in range(1, side):
        to = lax.rem(a + i, side)
        ga_out[to] = row_grads(last, to).astype(BF16)
        remote(ga_out.at[to], ga_in.at[a], GRAD_A, GRAD_A, to * a_step + b * b_step, e).start()
    sent.append((ga_in.at[pl.ds(0, side - 1)], GRAD_A))
    ga_in[a] = row_grads(last, a).astype(BF16)

    took(tower_a_in.at[pl.ds(0, side - 1)], rs.at[GIN_A])
    to_sibling(gin.at[core], gin.at[core], GIN_S)
    took(gto_e.at[pl.ds(0, n_expert - 1)], rs.at[GTO_E])
    gtout_ref[...] = sum_of(gto_e, n_expert)
    took(gin.at[0], rs.at[GIN_S])
    gin_outs = [
        pltpu.make_async_copy(gin.at[h], gin_hbm.at[:, pl.ds(h * t_cols, t_cols)], local_sem.at[3 + h]) for h in range(2)
    ]
    for copy in gin_outs:
        copy.start()

    took(ga_in.at[pl.ds(0, side - 1)], rs.at[GRAD_A])
    total = sum_of(ga_in, side)
    for k in range(side):
        gb_out[k] = total[:, k * span : (k + 1) * span].astype(BF16)
    fan_b(lambda to: gb_out.at[to], gb_in.at[b], GRAD_B, gb_in.at[pl.ds(0, side - 1)])
    gb_in[b] = gb_out[b]
    took(gb_in.at[pl.ds(0, side - 1)], rs.at[GRAD_B])
    gx_out[...] = sum_of(gb_in, side).T.astype(BF16).reshape(n_x, per, LANES)
    fan_x(lambda to: gx_out.at[to], gx_in.at[x], GRAD_X, gx_in.at[pl.ds(0, n_x - 1)])
    gx_in[x] = gx_out[x]
    took(gx_in.at[pl.ds(0, n_x - 1)], rs.at[GRAD_X])
    grows_ref[...] = sum_of(gx_in, n_x)

    for ref, k in sent:
        took(ref, ss.at[k])
    for copy in gin_outs:
        copy.wait()


def finish(gin_ref, grows_ref, gto_ref, gin_out, grows_out, gto_out):
    gin_out[...] = gin_ref[...].astype(F32)
    grows_out[...] = grows_ref[...]
    gto_out[...] = gto_ref[...]


def per_device(emb_rows, row_ids, route_ids, route_gates, w_in, w_out, tower_in, tower_out, labels):
    n_table = lax.axis_size("table")
    n_expert = lax.axis_size("expert")
    n_x = n_expert // 2
    side = math.isqrt(n_table)
    samples, tables, bag = row_ids.shape
    cap = 3 * samples // n_expert
    row_dev, dim = emb_rows.shape
    width = tables * dim
    hid, eout = w_out.shape[1:]
    tasks, tw = tower_out.shape
    per = row_dev // n_expert
    span = n_x * per
    cols = n_table * span
    slots = n_expert * cap
    n_chunks = width // CHUNK
    m_rows = slots // HALVES
    t_rows = eout // n_table
    t_cols = tasks * tw // 2
    x_cols = t_cols // n_x
    vmem = pl.BlockSpec(memory_space=pltpu.VMEM)
    hbm = pl.BlockSpec(memory_space=pl.ANY)
    dma = pltpu.SemaphoreType.DMA
    scratch = [
        pltpu.VMEM((width, hid), BF16),
        pltpu.VMEM((hid, eout), BF16),
        pltpu.VMEM((eout, tasks * tw), BF16),
        pltpu.VMEM((2, tables * bag, samples), jnp.int32),
        pltpu.VMEM((LANES, samples), F32),
        pltpu.VMEM((2, width, cols), BF16),
        pltpu.VMEM((side, side, span, LANES), BF16),
        pltpu.VMEM((n_chunks, CHUNK, LANES), F32),
        pltpu.VMEM((n_chunks, CHUNK, LANES), F32),
        pltpu.VMEM((2, samples, slots), BF16),
        pltpu.VMEM((samples, slots), BF16),
        pltpu.VMEM((slots, samples), BF16),
        pltpu.VMEM((slots, 2 * samples), BF16),
        pltpu.VMEM((n_chunks, n_expert, cap, CHUNK), BF16),
        pltpu.VMEM((n_chunks, n_expert, cap, CHUNK), BF16),
        pltpu.VMEM((m_rows, eout), F32),
        pltpu.VMEM((HALVES, m_rows, hid), BF16),
        pltpu.VMEM((n_expert, cap, eout), BF16),
        pltpu.VMEM((n_expert, cap, eout), BF16),
        pltpu.VMEM((2, samples, eout), BF16),
        pltpu.VMEM((2, samples, t_cols), BF16),
        pltpu.VMEM((2, samples, t_cols), BF16),
        pltpu.VMEM((eout, 2 * samples), BF16),
        pltpu.VMEM((side, side * t_rows, t_cols), BF16),
        pltpu.VMEM((side, side * t_rows, t_cols), BF16),
        pltpu.VMEM((side, t_rows, t_cols), BF16),
        pltpu.VMEM((side, t_rows, t_cols), BF16),
        pltpu.VMEM((n_x, t_rows, x_cols), BF16),
        pltpu.VMEM((n_x, t_rows, x_cols), BF16),
        pltpu.VMEM((2, eout, t_cols), BF16),
        pltpu.VMEM((3, tasks, tw), F32),
        pltpu.VMEM((side, tasks, tw), F32),
        pltpu.VMEM((side, tasks, tw), F32),
        pltpu.VMEM((n_expert, tasks, tw), F32),
        pltpu.VMEM((n_expert, cap, eout), BF16),
        pltpu.VMEM((n_expert, cap, eout), BF16),
        pltpu.VMEM((HALVES, m_rows, hid), BF16),
        pltpu.VMEM((n_chunks, n_expert, cap, CHUNK), BF16),
        pltpu.VMEM((n_chunks, n_expert, cap, CHUNK), BF16),
        pltpu.VMEM((n_chunks, 2, LANES, CHUNK), BF16),
        pltpu.VMEM((side, LANES, side * span), F32),
        pltpu.VMEM((side, LANES, side * span), BF16),
        pltpu.VMEM((side, LANES, side * span), BF16),
        pltpu.VMEM((side, LANES, span), BF16),
        pltpu.VMEM((side, LANES, span), BF16),
        pltpu.VMEM((n_x, per, LANES), BF16),
        pltpu.VMEM((n_x, per, LANES), BF16),
        dma((5,)),
        dma((N_SEMS,)),
        dma((N_SEMS,)),
    ]
    grows, gin, gtout = pl.pallas_call(
        functools.partial(kernel, n_table, n_expert),
        out_shape=(
            jax.ShapeDtypeStruct((per, dim), F32),
            jax.ShapeDtypeStruct((eout, tasks * tw), BF16),
            jax.ShapeDtypeStruct((tasks, tw), F32),
        ),
        in_specs=[vmem] * 6 + [hbm] * 3,
        out_specs=(vmem, hbm, vmem),
        scratch_shapes=scratch,
        compiler_params=pltpu.CompilerParams(
            collective_id=0, has_side_effects=True, vmem_limit_bytes=VMEM_LIMIT
        ),
    )(
        jnp.transpose(row_ids, (1, 2, 0)).reshape(tables * bag, samples),
        emb_rows.reshape(n_x, 2, per, dim),
        route_ids.T,
        route_gates.T,
        labels.T,
        tower_out,
        w_in[0],
        w_out[0],
        tower_in,
    )
    whole = lambda shape: pl.BlockSpec(shape, lambda i: (0, 0))
    piece = pl.BlockSpec((eout // 4, tasks * tw), lambda i: (i, 0))
    gin, grows, gtout = pl.pallas_call(
        finish,
        grid=(4,),
        out_shape=(
            jax.ShapeDtypeStruct((eout, tasks * tw), F32),
            jax.ShapeDtypeStruct((per, dim), F32),
            jax.ShapeDtypeStruct((tasks, tw), F32),
        ),
        in_specs=[piece, whole((per, dim)), whole((tasks, tw))],
        out_specs=(piece, whole((per, dim)), whole((tasks, tw))),
    )(gin, grows, gtout)
    return grows, gin, gtout


VMEM_LIMIT = 63 * 1024 * 1024


def solution(mesh):
    return jax.shard_map(
        per_device,
        mesh=mesh,
        in_specs=(
            P("table", None),
            P(("table", "expert"), None, None),
            P(("table", "expert"), None),
            P(("table", "expert"), None),
            P("expert", None, None),
            P("expert", None, None),
            P(),
            P(),
            P(("table", "expert"), None),
        ),
        out_specs=(P(("table", "expert"), None), P(), P()),
        check_vma=False,
    )
```

```python
import functools
import math

import jax
import jax.numpy as jnp
from jax import lax
from jax.experimental import pallas as pl
from jax.experimental.pallas import tpu as pltpu
from jax.sharding import PartitionSpec as P

MESH = pl.DeviceIdType.MESH
F32 = jnp.float32
BF16 = jnp.bfloat16
LANES = 128
HALVES = 2
CHUNK = 256
TILE = 2048


IDS, EMB_A, EMB_B, COMB, DTOW, GTO_A, GTO_B, GTO_E = range(8)
TOW_A, TOW_B, TOW_X, GIN_B, GIN_A, GIN_S = range(8, 14)
BACK, GRAD_A, GRAD_B, GRAD_X = range(15, 19)
DBOX = 20
PART = 24
DBACK = 28
DPOOL = 32
BOX = 36
N_SEMS = 40


def dot(a, b):
    return lax.dot_general(a, b, (((1,), (0,)), ((), ())), preferred_element_type=F32)


def dot_nt(a, b):
    return lax.dot_general(a, b, (((1,), (1,)), ((), ())), preferred_element_type=F32)


def silu_grad(pre, sig):
    return sig * (1.0 + pre * (1.0 - sig))


def kernel(
    n_table,
    n_expert,
    ids_ref,
    emb_ref,
    route_ref,
    gate_ref,
    labels_ref,
    tout_ref,
    w_in_hbm,
    w_out_hbm,
    tin_hbm,
    grows_ref,
    gin_hbm,
    gtout_ref,
    w_in,
    w_out,
    tin,
    ids,
    narrow,
    counts,
    rows,
    part_out,
    part_own,
    part_in,
    place,
    place_sum,
    place_t,
    place_both_t,
    outbox,
    inbox,
    acc,
    pre_acc,
    slope,
    made,
    returned,
    comb,
    dtow,
    dtow_own,
    comb_t,
    tower_a_out,
    tower_a_in,
    tower_b_out,
    tower_b_in,
    tower_x_out,
    tower_x_in,
    gin,
    gto_out,
    gto_a,
    gto_b,
    gto_e,
    dout,
    din,
    drows,
    dback,
    dpooled_t,
    grad_acc,
    ga_out,
    ga_in,
    gb_out,
    gb_in,
    gx_out,
    gx_in,
    local_sem,
    ss,
    rs,
):
    t = lax.axis_index("table")
    e = lax.axis_index("expert")
    n_x = n_expert // 2
    side = math.isqrt(n_table)
    x = e // 2
    core = e % 2
    sib = 1 - core
    first = core == 0
    a = jnp.where(first, t // side, t % side)
    b = jnp.where(first, t % side, t // side)
    a_step = jnp.where(first, side, 1)
    b_step = jnp.where(first, 1, side)
    lookups, batch = ids_ref.shape
    n_chunks = outbox.shape[0]
    width = n_chunks * CHUNK
    n_feat = width // LANES
    bag = lookups // n_feat
    cap = inbox.shape[2]
    slots = n_expert * cap
    hid = w_in.shape[1]
    eout = w_out.shape[1]
    tasks, tw = tout_ref.shape
    per = emb_ref.shape[2]
    span = n_x * per
    cols = n_table * span
    rel_per = n_expert // HALVES
    m_rows = rel_per * cap
    per_chunk = CHUNK // LANES

    far = n_x // 2
    rels = [(far, 0), (far, 1)]
    rels += [(d, 0) for d in range(1, n_x) if d != far]
    rels += [(0, 0), (0, 1)]
    rels += [(d, 1) for d in range(1, n_x) if d != far]
    me = rels.index((0, 0))
    others = [i for i in range(n_expert) if i != me]

    def rel_expert(i):
        d, c = rels[i]
        return lax.rem(x + d, n_x) * 2 + lax.rem(core + c, 2)

    def rel_back(i):
        d, c = rels[i]
        return rels.index(((n_x - d) % n_x, c))

    def remote(src, dst, k_send, k_recv, to_t, to_e):
        return pltpu.make_async_remote_copy(
            src_ref=src, dst_ref=dst, send_sem=ss.at[k_send], recv_sem=rs.at[k_recv],
            device_id=(to_t, to_e), device_id_type=MESH,
        )

    def took(ref, sem):
        pltpu.make_async_copy(ref, ref, sem).wait()

    sent = []

    def to_sibling(src, dst, k):
        remote(src, dst, k, k, t, x * 2 + sib).start()
        sent.append((src, k))

    def fan_a(src, dst, k, total):
        for i in range(1, side):
            to = lax.rem(a + i, side)
            remote(src(to), dst, k, k, to * a_step + b * b_step, e).start()
        sent.append((total, k))

    def fan_b(src, dst, k, total):
        for i in range(1, side):
            to = lax.rem(b + i, side)
            remote(src(to), dst, k, k, a * a_step + to * b_step, e).start()
        sent.append((total, k))

    def fan_x(src, dst, k, total):
        for i in range(1, n_x):
            to = lax.rem(x + i, n_x)
            remote(src(to), dst, k, k, t, to * 2 + core).start()
        sent.append((total, k))

    def sum_of(ref, n):
        total = ref[0].astype(F32)
        for i in range(1, n):
            total += ref[i].astype(F32)
        return total

    w_in_copy = pltpu.make_async_copy(w_in_hbm, w_in, local_sem.at[0])
    w_out_copy = pltpu.make_async_copy(w_out_hbm, w_out, local_sem.at[1])
    tin_copy = pltpu.make_async_copy(tin_hbm, tin, local_sem.at[2])

    barrier = pltpu.get_barrier_semaphore()
    for i in range(1, side):
        for to_t in (lax.rem(a + i, side) * a_step + b * b_step, a * a_step + lax.rem(b + i, side) * b_step):
            pl.semaphore_signal(barrier, inc=1, device_id=(to_t, e), device_id_type=MESH)
    for i in others:
        pl.semaphore_signal(barrier, inc=1, device_id=(t, rel_expert(i)), device_id_type=MESH)

    ids[0] = ids_ref[...]
    rows[b, a] = emb_ref[:, core].reshape(span, LANES)
    pl.semaphore_wait(barrier, 2 * (side - 1) + n_expert - 1)

    fan_a(lambda to: rows.at[b, a], rows.at[b, a], EMB_A, rows.at[0, pl.ds(0, side - 1)])
    to_sibling(ids.at[0], ids.at[1], IDS)
    w_in_copy.start()
    w_out_copy.start()
    tin_copy.start()

    narrow[...] = jnp.zeros_like(narrow)
    narrow[0:2] = route_ref[...].astype(F32)
    narrow[8:10] = gate_ref[...]
    narrow[16 : 16 + tasks] = labels_ref[...]
    columns = narrow[...].T
    lane = lax.broadcasted_iota(jnp.int32, (batch, LANES), 1)
    slot_lane = lax.broadcasted_iota(jnp.int32, (batch, slots), 1)
    r0, r1 = columns[:, 0:1].astype(jnp.int32), columns[:, 1:2].astype(jnp.int32)
    gate0, gate1 = columns[:, 8:9], columns[:, 9:10]
    named0, named1 = lane == r0, lane == r1
    named = jnp.where(named0 | named1, 1.0, 0.0).astype(BF16)
    earlier = jnp.where(
        lax.broadcasted_iota(jnp.int32, (batch, batch), 1) < lax.broadcasted_iota(jnp.int32, (batch, batch), 0),
        1.0, 0.0,
    ).astype(BF16)
    before = dot(earlier, named)
    placed = []
    for j, (r, hit) in enumerate(((r0, named0), (r1, named1))):
        pos = jnp.sum(jnp.where(hit, before, 0.0), axis=1, keepdims=True).astype(jnp.int32)
        placed.append(jnp.where(slot_lane == r * cap + pos, 1.0, 0.0))
        place[j] = placed[j].astype(BF16)
        place_both_t[:, j * batch : (j + 1) * batch] = placed[j].T.astype(BF16)
    both = placed[0] + placed[1]
    place_sum[...] = both.astype(BF16)
    place_t[...] = both.T.astype(BF16)

    def code_of(s):
        own = ids[s]
        shard = own // (n_x * 2 * per)
        near = lax.rem(own // (2 * per), n_x) * per + lax.rem(own, per)
        at_a = jnp.where(first, shard // side, lax.rem(shard, side))
        at_b = jnp.where(first, lax.rem(shard, side), shard // side)
        code = jnp.where(lax.rem(own // per, 2) == core, (at_b * side + at_a) * span + near, -1)
        flat = jnp.concatenate([code.astype(F32), jnp.zeros((LANES - lookups, batch), F32)], axis=0)
        return flat.T.astype(jnp.int32)

    def build_counts(s, code, features):
        for f in features:
            words = [jnp.zeros((batch, LANES), jnp.int32) for _ in range(-(-cols // (8 * LANES)))]
            for k in range(bag):
                c = f * bag + k
                gap = code[:, c : c + 1] - lane
                high = gap >> 7
                one = jnp.where(jnp.bitwise_and(gap, LANES - 1) == 0, 1 << (jnp.bitwise_and(high, 7) * 4), 0)
                which = high >> 3
                for w in range(len(words)):
                    words[w] = words[w] + jnp.where(which == w, one, 0)
            for h in range(cols // LANES):
                count = jnp.bitwise_and(words[h // 8] >> (4 * (h % 8)), 15)
                counts[s, f * batch : (f + 1) * batch, h * LANES : (h + 1) * LANES] = count.astype(F32).astype(BF16)

    code = code_of(0)
    build_counts(0, code, range(n_feat // 2))
    took(rows.at[0, pl.ds(0, side - 1)], rs.at[EMB_A])
    fan_b(lambda to: rows.at[b], rows.at[b], EMB_B, rows.at[pl.ds(0, side - 1)])
    build_counts(0, code, range(n_feat // 2, n_feat))
    took(ids.at[1], rs.at[IDS])
    build_counts(1, code_of(1), range(n_feat))

    part_cols = side * span

    def partial(s, c, at_b):
        at = pl.ds(pl.multiple_of(at_b * part_cols, part_cols), part_cols)
        return dot(counts[s, c * CHUNK : (c + 1) * CHUNK, at], rows[at_b].reshape(part_cols, LANES))

    for c in range(n_chunks):
        part_out[c] = partial(1, c, b)
        part_own[c] = partial(0, c, b)
    took(rows.at[pl.ds(0, side - 1)], rs.at[EMB_B])

    def all_parts(s, c, total):
        for i in range(1, side):
            total += partial(s, c, lax.rem(b + i, side))
        return total

    def swap_partial(c):
        part_out[c] = all_parts(1, c, part_out[c])
        to_sibling(part_out.at[c], part_in.at[c], PART + c)

    swap_partial(0)
    for c in range(n_chunks):
        mine = all_parts(0, c, part_own[c])
        if c + 1 < n_chunks:
            swap_partial(c + 1)
        took(part_in.at[c], rs.at[PART + c])
        pooled = (mine + part_in[c]).astype(BF16)
        tokens = jnp.concatenate([pooled[f * batch : (f + 1) * batch] for f in range(per_chunk)], axis=1)
        outbox[c] = dot(place_t[...], tokens).astype(BF16).reshape(n_expert, cap, CHUNK)
        for i in others:
            to = rel_expert(i)
            remote(outbox.at[c, to], inbox.at[c, rel_back(i)], BOX + c, BOX + c, t, to).start()
        sent.append((outbox.at[c, pl.ds(0, n_expert - 1)], BOX + c))
        inbox[c, me] = outbox[c, e]

    w_in_copy.wait()
    w_out_copy.wait()

    def arrived(half):
        return pl.ds(half * rel_per, rel_per - (me // rel_per == half))

    tile = min(TILE, hid)

    for c in range(n_chunks - 1):
        took(inbox.at[c, pl.ds(0, n_expert - 1)], rs.at[BOX + c])

        @pl.loop(0, hid // tile)
        def _(n):
            at = pl.ds(pl.multiple_of(n * tile, tile), tile)
            pre = dot(inbox[c].reshape(slots, CHUNK), w_in[c * CHUNK : (c + 1) * CHUNK, at])
            pre_acc[:, at] = pre if c == 0 else pre_acc[:, at] + pre

    last = n_chunks - 1
    took(inbox.at[last, pl.ds(0, n_expert - 1)], rs.at[BOX + last])
    for half in range(HALVES):
        acc[...] = jnp.zeros_like(acc)
        mine = slice(half * rel_per, (half + 1) * rel_per)

        @pl.loop(0, hid // tile)
        def _(n):
            at = pl.ds(pl.multiple_of(n * tile, tile), tile)
            pre = dot(inbox[last, mine].reshape(m_rows, CHUNK), w_in[last * CHUNK : (last + 1) * CHUNK, at])
            pre += pre_acc[half * m_rows : (half + 1) * m_rows, at]
            sig = jax.nn.sigmoid(pre)
            slope[half, :, at] = silu_grad(pre, sig).astype(BF16)
            acc[...] += dot((pre * sig).astype(BF16), w_out[at, :])

        made[mine] = acc[...].astype(BF16).reshape(rel_per, cap, eout)
        for i in others:
            if i // rel_per == half:
                remote(made.at[i], returned.at[e], BACK, BACK, t, rel_expert(i)).start()

    sent.append((made.at[pl.ds(0, n_expert - 1)], BACK))
    returned[e] = made[me]
    tin_copy.wait()
    took(returned.at[pl.ds(0, n_expert - 1)], rs.at[BACK])

    answers = returned[...].reshape(slots, eout)
    combined = (gate0 * dot(place[0], answers) + gate1 * dot(place[1], answers)).astype(BF16)
    comb[0] = combined
    per_half = tasks // 2
    for k in range(tasks):
        pre = dot(combined, tin[:, k * tw : (k + 1) * tw])
        sig = jax.nn.sigmoid(pre)
        units = pre * sig
        out_row = tout_ref[k : k + 1, :]
        logit = jnp.sum(units * out_row, axis=1, keepdims=True)
        dlogit = (jax.nn.sigmoid(logit) - columns[:, 16 + k : 17 + k]) / tasks
        gto_out[0, k : k + 1, :] = jnp.sum(dlogit * units, axis=0, keepdims=True)
        grad = (dlogit * out_row * silu_grad(pre, sig)).astype(BF16)
        dtow[k // per_half, :, (k % per_half) * tw : (k % per_half + 1) * tw] = grad
    to_sibling(comb.at[0], comb.at[1], COMB)
    to_sibling(dtow.at[sib], dtow_own.at[1], DTOW)
    dcomb = sum(dot_nt(dtow[h], tin[:, h * per_half * tw : (h + 1) * per_half * tw]) for h in range(2))
    dent = jnp.concatenate([(gate0 * dcomb).astype(BF16), (gate1 * dcomb).astype(BF16)], axis=0)
    dout[...] = dot(place_both_t[...], dent).astype(BF16).reshape(n_expert, cap, eout)
    for i in reversed(others):
        at = rel_back(i)
        to = rel_expert(i)
        remote(dout.at[to], din.at[at], DBOX, DBOX + at // rel_per, t, to).start()
    sent.append((dout.at[pl.ds(0, n_expert - 1)], DBOX))
    din[me] = dout[e]

    fan_a(lambda to: gto_out.at[0], gto_a.at[a], GTO_A, gto_a.at[pl.ds(0, side - 1)])
    gto_a[a] = gto_out[0]
    dtow_own[0] = dtow[core]
    comb_t[:, 0:batch] = comb[0].astype(F32).T.astype(BF16)
    took(comb.at[1], rs.at[COMB])
    took(dtow_own.at[1], rs.at[DTOW])
    comb_t[:, batch : 2 * batch] = comb[1].astype(F32).T.astype(BF16)
    t_rows = eout // n_table
    t_cols = tasks * tw // 2
    big = side * t_rows

    @pl.loop(0, side)
    def _(i):
        block = dot(comb_t[pl.ds(pl.multiple_of(i * big, big), big), :], dtow_own[...].reshape(2 * batch, t_cols))
        tower_a_out[i] = block.astype(BF16)

    fan_a(lambda to: tower_a_out.at[to], tower_a_in.at[a], TOW_A, tower_a_in.at[pl.ds(0, side - 1)])
    tower_a_in[a] = tower_a_out[a]

    def tower_first():
        took(tower_a_in.at[pl.ds(0, side - 1)], rs.at[TOW_A])
        took(gto_a.at[pl.ds(0, side - 1)], rs.at[GTO_A])
        tower_b_out[...] = sum_of(tower_a_in, side).astype(BF16).reshape(side, t_rows, t_cols)
        fan_b(lambda to: tower_b_out.at[to], tower_b_in.at[b], TOW_B, tower_b_in.at[pl.ds(0, side - 1)])
        tower_b_in[b] = tower_b_out[b]
        gto_out[1] = sum_of(gto_a, side)
        fan_b(lambda to: gto_out.at[1], gto_b.at[b], GTO_B, gto_b.at[pl.ds(0, side - 1)])
        gto_b[b] = gto_out[1]

    for half in reversed(range(HALVES)):
        took(din.at[arrived(half)], rs.at[DBOX + half])
        if half == 0:
            tower_first()
        mine = slice(half * rel_per, (half + 1) * rel_per)

        @pl.loop(0, hid // tile)
        def _(n):
            at = pl.ds(pl.multiple_of(n * tile, tile), tile)
            dhid = dot_nt(din[mine].reshape(m_rows, eout), w_out[at, :])
            slope[half, :, at] = (dhid * slope[half, :, at].astype(F32)).astype(BF16)

    def token_grads(c):
        for half in range(HALVES):
            block = dot_nt(slope[half], w_in[c * CHUNK : (c + 1) * CHUNK, :])
            drows[c, half * rel_per : (half + 1) * rel_per] = block.astype(BF16).reshape(rel_per, cap, CHUNK)
        for i in others:
            remote(drows.at[c, i], dback.at[c, e], DBACK + c, DBACK + c, t, rel_expert(i)).start()
        sent.append((drows.at[c, pl.ds(0, n_expert - 1)], DBACK + c))
        dback[c, e] = drows[c, me]

    def pooled_grads(c):
        took(dback.at[c, pl.ds(0, n_expert - 1)], rs.at[DBACK + c])
        got = dot(place_sum[...], dback[c].reshape(slots, CHUNK)).astype(BF16).astype(F32)
        for f in range(per_chunk):
            dpooled_t[c, 0, :, f * batch : (f + 1) * batch] = got[:, f * LANES : (f + 1) * LANES].T.astype(BF16)
        to_sibling(dpooled_t.at[c, 0], dpooled_t.at[c, 1], DPOOL + c)

    def row_grads(c, at_a):
        total = None
        for s in range(2):
            parts = [
                counts[s, c * CHUNK : (c + 1) * CHUNK, pl.ds(pl.multiple_of((bb * side + at_a) * span, span), span)]
                for bb in range(side)
            ]
            term = dot(dpooled_t[c, s], jnp.concatenate(parts, axis=1))
            total = term if total is None else total + term
        return total if c == 0 else total + grad_acc[at_a]

    def add_chunk(c):
        took(dpooled_t.at[c, 1], rs.at[DPOOL + c])
        for at_a in range(side):
            grad_acc[at_a] = row_grads(c, at_a)

    def gin_rows(at, n):
        return pl.ds(pl.multiple_of(at * t_rows, t_rows), n * t_rows)

    my_rows, my_big = gin_rows(a * side + b, 1), gin_rows(a * side, side)

    def tower_second():
        took(tower_b_in.at[pl.ds(0, side - 1)], rs.at[TOW_B])
        took(gto_b.at[pl.ds(0, side - 1)], rs.at[GTO_B])
        tower_x_out[...] = sum_of(tower_b_in, side).astype(BF16)
        fan_x(lambda to: tower_x_out, tower_x_in.at[x], TOW_X, tower_x_in.at[pl.ds(0, n_x - 1)])
        tower_x_in[x] = tower_x_out[...]
        gto_out[2] = sum_of(gto_b, side)
        for i in others:
            remote(gto_out.at[2], gto_e.at[e], GTO_E, GTO_E, t, rel_expert(i)).start()
        sent.append((gto_e.at[pl.ds(0, n_expert - 1)], GTO_E))
        gto_e[e] = gto_out[2]

    def tower_x():
        took(tower_x_in.at[pl.ds(0, n_x - 1)], rs.at[TOW_X])
        gin[core, my_rows] = sum_of(tower_x_in, n_x).astype(BF16)
        block = gin.at[core, my_rows]
        fan_b(lambda to: block, block, GIN_B, tower_b_in.at[pl.ds(0, side - 1)])

    def gather_b():
        took(tower_b_in.at[pl.ds(0, side - 1)], rs.at[GIN_B])
        block = gin.at[core, my_big]
        fan_a(lambda to: block, block, GIN_A, tower_a_in.at[pl.ds(0, side - 1)])

    beside = {0: tower_second, 3: tower_x}
    for c in range(n_chunks):
        token_grads(c)
        if c in beside:
            beside[c]()
    beside = {1: gather_b}
    for c in range(n_chunks):
        pooled_grads(c)
        if c > 0:
            add_chunk(c - 1)
        if c in beside:
            beside[c]()

    took(dpooled_t.at[last, 1], rs.at[DPOOL + last])
    for i in range(1, side):
        to = lax.rem(a + i, side)
        ga_out[to] = row_grads(last, to).astype(BF16)
        remote(ga_out.at[to], ga_in.at[a], GRAD_A, GRAD_A, to * a_step + b * b_step, e).start()
    sent.append((ga_in.at[pl.ds(0, side - 1)], GRAD_A))
    ga_in[a] = row_grads(last, a).astype(BF16)

    took(ga_in.at[pl.ds(0, side - 1)], rs.at[GRAD_A])
    total = sum_of(ga_in, side)
    for k in range(side):
        gb_out[k] = total[:, k * span : (k + 1) * span].astype(BF16)
    fan_b(lambda to: gb_out.at[to], gb_in.at[b], GRAD_B, gb_in.at[pl.ds(0, side - 1)])
    gb_in[b] = gb_out[b]
    took(tower_a_in.at[pl.ds(0, side - 1)], rs.at[GIN_A])
    to_sibling(gin.at[core], gin.at[core], GIN_S)
    took(gto_e.at[pl.ds(0, n_expert - 1)], rs.at[GTO_E])
    gtout_ref[...] = sum_of(gto_e, n_expert)
    took(gb_in.at[pl.ds(0, side - 1)], rs.at[GRAD_B])
    gx_out[...] = sum_of(gb_in, side).T.astype(BF16).reshape(n_x, per, LANES)
    fan_x(lambda to: gx_out.at[to], gx_in.at[x], GRAD_X, gx_in.at[pl.ds(0, n_x - 1)])
    gx_in[x] = gx_out[x]
    took(gin.at[0], rs.at[GIN_S])
    gin_outs = [
        pltpu.make_async_copy(gin.at[h], gin_hbm.at[:, pl.ds(h * t_cols, t_cols)], local_sem.at[3 + h]) for h in range(2)
    ]
    for copy in gin_outs:
        copy.start()
    took(gx_in.at[pl.ds(0, n_x - 1)], rs.at[GRAD_X])
    grows_ref[...] = sum_of(gx_in, n_x)

    for ref, k in sent:
        took(ref, ss.at[k])
    for copy in gin_outs:
        copy.wait()


def finish(gin_hbm, grows_hbm, gto_hbm, gin_out, grows_out, gto_out, narrow, wide, sem_in, sem_out):
    n = sem_in.shape[0] - 2
    step = narrow.shape[0] // n
    pieces = [pl.ds(i * step, step) for i in range(n)]
    ins = [pltpu.make_async_copy(gin_hbm.at[p], narrow.at[p], sem_in.at[i]) for i, p in enumerate(pieces)]
    outs = [pltpu.make_async_copy(wide.at[p], gin_out.at[p], sem_out.at[i]) for i, p in enumerate(pieces)]
    small = [
        pltpu.make_async_copy(grows_hbm, grows_out, sem_in.at[n]),
        pltpu.make_async_copy(gto_hbm, gto_out, sem_in.at[n + 1]),
    ]
    for copy in ins + small:
        copy.start()
    for i, p in enumerate(pieces):
        ins[i].wait()
        wide[p] = narrow[p].astype(F32)
        outs[i].start()
    for copy in outs + small:
        copy.wait()


def per_device(emb_rows, row_ids, route_ids, route_gates, w_in, w_out, tower_in, tower_out, labels):
    n_table = lax.axis_size("table")
    n_expert = lax.axis_size("expert")
    n_x = n_expert // 2
    side = math.isqrt(n_table)
    samples, tables, bag = row_ids.shape
    cap = 3 * samples // n_expert
    row_dev, dim = emb_rows.shape
    width = tables * dim
    hid, eout = w_out.shape[1:]
    tasks, tw = tower_out.shape
    per = row_dev // n_expert
    span = n_x * per
    cols = n_table * span
    slots = n_expert * cap
    n_chunks = width // CHUNK
    m_rows = slots // HALVES
    t_rows = eout // n_table
    t_cols = tasks * tw // 2
    vmem = pl.BlockSpec(memory_space=pltpu.VMEM)
    hbm = pl.BlockSpec(memory_space=pl.ANY)
    dma = pltpu.SemaphoreType.DMA
    scratch = [
        pltpu.VMEM((width, hid), BF16),
        pltpu.VMEM((hid, eout), BF16),
        pltpu.VMEM((eout, tasks * tw), BF16),
        pltpu.VMEM((2, tables * bag, samples), jnp.int32),
        pltpu.VMEM((LANES, samples), F32),
        pltpu.VMEM((2, width, cols), BF16),
        pltpu.VMEM((side, side, span, LANES), BF16),
        pltpu.VMEM((n_chunks, CHUNK, LANES), F32),
        pltpu.VMEM((n_chunks, CHUNK, LANES), F32),
        pltpu.VMEM((n_chunks, CHUNK, LANES), F32),
        pltpu.VMEM((2, samples, slots), BF16),
        pltpu.VMEM((samples, slots), BF16),
        pltpu.VMEM((slots, samples), BF16),
        pltpu.VMEM((slots, 2 * samples), BF16),
        pltpu.VMEM((n_chunks, n_expert, cap, CHUNK), BF16),
        pltpu.VMEM((n_chunks, n_expert, cap, CHUNK), BF16),
        pltpu.VMEM((m_rows, eout), F32),
        pltpu.VMEM((slots, hid), F32),
        pltpu.VMEM((HALVES, m_rows, hid), BF16),
        pltpu.VMEM((n_expert, cap, eout), BF16),
        pltpu.VMEM((n_expert, cap, eout), BF16),
        pltpu.VMEM((2, samples, eout), BF16),
        pltpu.VMEM((2, samples, t_cols), BF16),
        pltpu.VMEM((2, samples, t_cols), BF16),
        pltpu.VMEM((eout, 2 * samples), BF16),
        pltpu.VMEM((side, side * t_rows, t_cols), BF16),
        pltpu.VMEM((side, side * t_rows, t_cols), BF16),
        pltpu.VMEM((side, t_rows, t_cols), BF16),
        pltpu.VMEM((side, t_rows, t_cols), BF16),
        pltpu.VMEM((t_rows, t_cols), BF16),
        pltpu.VMEM((n_x, t_rows, t_cols), BF16),
        pltpu.VMEM((2, eout, t_cols), BF16),
        pltpu.VMEM((3, tasks, tw), F32),
        pltpu.VMEM((side, tasks, tw), F32),
        pltpu.VMEM((side, tasks, tw), F32),
        pltpu.VMEM((n_expert, tasks, tw), F32),
        pltpu.VMEM((n_expert, cap, eout), BF16),
        pltpu.VMEM((n_expert, cap, eout), BF16),
        pltpu.VMEM((n_chunks, n_expert, cap, CHUNK), BF16),
        pltpu.VMEM((n_chunks, n_expert, cap, CHUNK), BF16),
        pltpu.VMEM((n_chunks, 2, LANES, CHUNK), BF16),
        pltpu.VMEM((side, LANES, side * span), F32),
        pltpu.VMEM((side, LANES, side * span), BF16),
        pltpu.VMEM((side, LANES, side * span), BF16),
        pltpu.VMEM((side, LANES, span), BF16),
        pltpu.VMEM((side, LANES, span), BF16),
        pltpu.VMEM((n_x, per, LANES), BF16),
        pltpu.VMEM((n_x, per, LANES), BF16),
        dma((5,)),
        dma((N_SEMS,)),
        dma((N_SEMS,)),
    ]
    grows, gin, gtout = pl.pallas_call(
        functools.partial(kernel, n_table, n_expert),
        out_shape=(
            jax.ShapeDtypeStruct((per, dim), F32),
            jax.ShapeDtypeStruct((eout, tasks * tw), BF16),
            jax.ShapeDtypeStruct((tasks, tw), F32),
        ),
        in_specs=[vmem] * 6 + [hbm] * 3,
        out_specs=(vmem, hbm, vmem),
        scratch_shapes=scratch,
        compiler_params=pltpu.CompilerParams(
            collective_id=0, has_side_effects=True, vmem_limit_bytes=VMEM_LIMIT
        ),
    )(
        jnp.transpose(row_ids, (1, 2, 0)).reshape(tables * bag, samples),
        emb_rows.reshape(n_x, 2, per, dim),
        route_ids.T,
        route_gates.T,
        labels.T,
        tower_out,
        w_in[0],
        w_out[0],
        tower_in,
    )
    gin, grows, gtout = pl.pallas_call(
        finish,
        out_shape=(
            jax.ShapeDtypeStruct((eout, tasks * tw), F32),
            jax.ShapeDtypeStruct((per, dim), F32),
            jax.ShapeDtypeStruct((tasks, tw), F32),
        ),
        in_specs=[hbm] * 3,
        out_specs=(hbm,) * 3,
        scratch_shapes=[
            pltpu.VMEM((eout, tasks * tw), BF16),
            pltpu.VMEM((eout, tasks * tw), F32),
            dma((10,)),
            dma((8,)),
        ],
    )(gin, grows, gtout)
    return grows, gin, gtout


VMEM_LIMIT = 63 * 1024 * 1024


def solution(mesh):
    return jax.shard_map(
        per_device,
        mesh=mesh,
        in_specs=(
            P("table", None),
            P(("table", "expert"), None, None),
            P(("table", "expert"), None),
            P(("table", "expert"), None),
            P("expert", None, None),
            P("expert", None, None),
            P(),
            P(),
            P(("table", "expert"), None),
        ),
        out_specs=(P(("table", "expert"), None), P(), P()),
        check_vma=False,
    )
```

```python
import functools
import math

import jax
import jax.numpy as jnp
from jax import lax
from jax.experimental import pallas as pl
from jax.experimental.pallas import tpu as pltpu
from jax.sharding import PartitionSpec as P

MESH = pl.DeviceIdType.MESH
F32 = jnp.float32
BF16 = jnp.bfloat16
LANES = 128
HALVES = 2
CHUNK = 256
WIDE = 512
TILE = 4096


IDS, EMB_A, EMB_B, COMB, DTOW, GTO_A, GTO_B, GTO_E = range(8)
TOW_A, TOW_B, TOW_X, GIN_B, GIN_X = range(8, 13)
BACK, GRAD_A, GRAD_B, GRAD_X = range(15, 19)
DBOX = 20
PART = 24
DBACK = 28
DPOOL = 32
BOX = 36
GIN_A = 40
GIN_S = 44
N_SEMS = 48


def dot(a, b):
    return lax.dot_general(a, b, (((1,), (0,)), ((), ())), preferred_element_type=F32)


def dot_nt(a, b):
    return lax.dot_general(a, b, (((1,), (1,)), ((), ())), preferred_element_type=F32)


def silu_and_slope(pre):
    sig = 0.5 * jnp.tanh(0.5 * pre) + 0.5
    out = pre * sig
    return out, sig + out * (1.0 - sig)


def kernel(
    n_table,
    n_expert,
    ids_hbm,
    emb_hbm,
    route_hbm,
    gate_hbm,
    labels_hbm,
    tout_hbm,
    w_in_hbm,
    w_out_hbm,
    tin_hbm,
    grows_hbm,
    gin_hbm,
    gtout_hbm,
    w_in,
    w_out,
    tin,
    ids,
    route,
    narrow,
    tout,
    grows,
    gtout,
    counts,
    rows,
    part_out,
    part_own,
    part_in,
    place,
    place_sum,
    place_t,
    place_both_t,
    outbox,
    inbox,
    acc,
    pre_acc,
    slope,
    made,
    returned,
    comb,
    dtow,
    dtow_own,
    comb_t,
    tower_a_out,
    tower_a_in,
    tower_b_out,
    tower_b_in,
    tower_x_out,
    tower_x_in,
    gin,
    gto_out,
    gto_a,
    gto_b,
    gto_e,
    dout,
    din,
    drows,
    dback,
    dpooled_t,
    grad_acc,
    ga_out,
    ga_in,
    gb_out,
    gb_in,
    gx_out,
    gx_in,
    local_sem,
    ss,
    rs,
):
    t = lax.axis_index("table")
    e = lax.axis_index("expert")
    n_x = n_expert // 2
    side = math.isqrt(n_table)
    x = e // 2
    core = e % 2
    sib = 1 - core
    first = core == 0
    a = jnp.where(first, t // side, t % side)
    b = jnp.where(first, t % side, t // side)
    a_step = jnp.where(first, side, 1)
    b_step = jnp.where(first, 1, side)
    lookups, batch = ids.shape[1:]
    n_chunks = outbox.shape[0]
    width = n_chunks * CHUNK
    n_feat = width // LANES
    bag = lookups // n_feat
    cap = inbox.shape[2]
    slots = n_expert * cap
    hid = w_in.shape[1]
    eout = w_out.shape[1]
    tasks, tw = tout.shape
    per = rows.shape[3]
    span = n_x * per
    cols = n_table * span
    rel_per = n_expert // HALVES
    m_rows = rel_per * cap
    per_chunk = CHUNK // LANES

    far = n_x // 2
    rels = [(far, 0), (far, 1)]
    rels += [(d, 0) for d in range(1, n_x) if d != far]
    rels += [(0, 0), (0, 1)]
    rels += [(d, 1) for d in range(1, n_x) if d != far]
    me = rels.index((0, 0))
    others = [i for i in range(n_expert) if i != me]

    def rel_expert(i):
        d, c = rels[i]
        return lax.rem(x + d, n_x) * 2 + lax.rem(core + c, 2)

    def rel_back(i):
        d, c = rels[i]
        return rels.index(((n_x - d) % n_x, c))

    def remote(src, dst, k_send, k_recv, to_t, to_e):
        return pltpu.make_async_remote_copy(
            src_ref=src, dst_ref=dst, send_sem=ss.at[k_send], recv_sem=rs.at[k_recv],
            device_id=(to_t, to_e), device_id_type=MESH,
        )

    def took(ref, sem):
        pltpu.make_async_copy(ref, ref, sem).wait()

    sent = []

    def to_sibling(src, dst, k):
        remote(src, dst, k, k, t, x * 2 + sib).start()
        sent.append((src, k))

    def fan_a(src, dst, k, total):
        for i in range(1, side):
            to = lax.rem(a + i, side)
            remote(src(to), dst, k, k, to * a_step + b * b_step, e).start()
        sent.append((total, k))

    def fan_b(src, dst, k, total):
        for i in range(1, side):
            to = lax.rem(b + i, side)
            remote(src(to), dst, k, k, a * a_step + to * b_step, e).start()
        sent.append((total, k))

    def fan_x(src, dst, k, total):
        for i in range(1, n_x):
            to = lax.rem(x + i, n_x)
            remote(src(to), dst, k, k, t, to * 2 + core).start()
        sent.append((total, k))

    def sum_of(ref, n):
        total = ref[0].astype(F32)
        for i in range(1, n):
            total += ref[i].astype(F32)
        return total

    barrier = pltpu.get_barrier_semaphore()
    for i in range(1, side):
        for to_t in (lax.rem(a + i, side) * a_step + b * b_step, a * a_step + lax.rem(b + i, side) * b_step):
            pl.semaphore_signal(barrier, inc=1, device_id=(to_t, e), device_id_type=MESH)
    for i in others:
        pl.semaphore_signal(barrier, inc=1, device_id=(t, rel_expert(i)), device_id_type=MESH)

    def local(src, dst, k):
        return pltpu.make_async_copy(src, dst, local_sem.at[k])

    ids_copy = local(ids_hbm, ids.at[0], 0)
    emb_copy = local(emb_hbm.at[:, core], rows.at[b, a], 1)
    small = [
        local(route_hbm, route, 2),
        local(gate_hbm, narrow.at[pl.ds(0, 2)], 3),
        local(labels_hbm, narrow.at[pl.ds(8, tasks)], 4),
        local(tout_hbm, tout, 5),
    ]
    w_in_copy = local(w_in_hbm, w_in, 6)
    w_out_copy = local(w_out_hbm, w_out, 7)
    tin_copy = local(tin_hbm, tin, 8)
    for copy in [emb_copy, ids_copy] + small:
        copy.start()
    emb_copy.wait()
    ids_copy.wait()
    pl.semaphore_wait(barrier, 2 * (side - 1) + n_expert - 1)

    fan_a(lambda to: rows.at[b, a], rows.at[b, a], EMB_A, rows.at[0, pl.ds(0, side - 1)])
    to_sibling(ids.at[0], ids.at[1], IDS)
    w_in_copy.start()
    w_out_copy.start()
    tin_copy.start()

    for copy in small:
        copy.wait()
    columns = narrow[...].T
    named_by = jnp.concatenate([route[...].astype(F32), jnp.zeros((LANES - 2, batch), F32)], axis=0).T.astype(jnp.int32)
    lane = lax.broadcasted_iota(jnp.int32, (batch, LANES), 1)
    slot_lane = lax.broadcasted_iota(jnp.int32, (batch, slots), 1)
    r0, r1 = named_by[:, 0:1], named_by[:, 1:2]
    gate0, gate1 = columns[:, 0:1], columns[:, 1:2]
    named0, named1 = lane == r0, lane == r1
    named = jnp.where(named0 | named1, 1.0, 0.0).astype(BF16)
    earlier = jnp.where(
        lax.broadcasted_iota(jnp.int32, (batch, batch), 1) < lax.broadcasted_iota(jnp.int32, (batch, batch), 0),
        1.0, 0.0,
    ).astype(BF16)
    before = dot(earlier, named)
    placed = []
    for j, (r, hit) in enumerate(((r0, named0), (r1, named1))):
        pos = jnp.sum(jnp.where(hit, before, 0.0), axis=1, keepdims=True).astype(jnp.int32)
        placed.append(jnp.where(slot_lane == r * cap + pos, 1.0, 0.0))
        place[j] = placed[j].astype(BF16)
        place_both_t[:, j * batch : (j + 1) * batch] = placed[j].T.astype(BF16)
    both = placed[0] + placed[1]
    place_sum[...] = both.astype(BF16)
    place_t[...] = both.T.astype(BF16)

    def code_of(s):
        own = ids[s]
        shard = own // (n_x * 2 * per)
        near = lax.rem(own // (2 * per), n_x) * per + lax.rem(own, per)
        at_a = jnp.where(first, shard // side, lax.rem(shard, side))
        at_b = jnp.where(first, lax.rem(shard, side), shard // side)
        code = jnp.where(lax.rem(own // per, 2) == core, (at_b * side + at_a) * span + near, -1)
        flat = jnp.concatenate([code.astype(F32), jnp.zeros((LANES - lookups, batch), F32)], axis=0)
        return flat.T.astype(jnp.int32)

    def build_counts(s, code, features):
        for f in features:
            words = [jnp.zeros((batch, LANES), jnp.int32) for _ in range(-(-cols // (8 * LANES)))]
            for k in range(bag):
                c = f * bag + k
                gap = code[:, c : c + 1] - lane
                high = gap >> 7
                one = jnp.where(jnp.bitwise_and(gap, LANES - 1) == 0, 1 << (jnp.bitwise_and(high, 7) * 4), 0)
                which = high >> 3
                for w in range(len(words)):
                    words[w] = words[w] + jnp.where(which == w, one, 0)
            for h in range(cols // LANES):
                count = jnp.bitwise_and(words[h // 8] >> (4 * (h % 8)), 15)
                counts[s, f * batch : (f + 1) * batch, h * LANES : (h + 1) * LANES] = count.astype(F32).astype(BF16)

    code = code_of(0)
    build_counts(0, code, range(n_feat // 2))
    took(rows.at[0, pl.ds(0, side - 1)], rs.at[EMB_A])
    fan_b(lambda to: rows.at[b], rows.at[b], EMB_B, rows.at[pl.ds(0, side - 1)])
    build_counts(0, code, range(n_feat // 2, n_feat))
    took(ids.at[1], rs.at[IDS])
    build_counts(1, code_of(1), range(n_feat))

    part_cols = side * span

    def partial(s, c, at_b):
        at = pl.ds(pl.multiple_of(at_b * part_cols, part_cols), part_cols)
        return dot(counts[s, c * CHUNK : (c + 1) * CHUNK, at], rows[at_b].reshape(part_cols, LANES))

    for c in range(n_chunks):
        part_out[c] = partial(1, c, b)
        part_own[c] = partial(0, c, b)
    took(rows.at[pl.ds(0, side - 1)], rs.at[EMB_B])

    def all_parts(s, c, total):
        for i in range(1, side):
            total += partial(s, c, lax.rem(b + i, side))
        return total

    def swap_partial(c):
        part_out[c] = all_parts(1, c, part_out[c])
        to_sibling(part_out.at[c], part_in.at[c], PART + c)

    swap_partial(0)
    for c in range(n_chunks):
        mine = all_parts(0, c, part_own[c])
        if c + 1 < n_chunks:
            swap_partial(c + 1)
        took(part_in.at[c], rs.at[PART + c])
        pooled = (mine + part_in[c]).astype(BF16)
        tokens = jnp.concatenate([pooled[f * batch : (f + 1) * batch] for f in range(per_chunk)], axis=1)
        outbox[c] = dot(place_t[...], tokens).astype(BF16).reshape(n_expert, cap, CHUNK)
        for i in others:
            to = rel_expert(i)
            remote(outbox.at[c, to], inbox.at[c, rel_back(i)], BOX + c, BOX + c, t, to).start()
        sent.append((outbox.at[c, pl.ds(0, n_expert - 1)], BOX + c))
        inbox[c, me] = outbox[c, e]

    w_in_copy.wait()
    w_out_copy.wait()

    def arrived(half):
        return pl.ds(half * rel_per, rel_per - (me // rel_per == half))

    tile = min(TILE, hid)

    for c in range(n_chunks - 1):
        took(inbox.at[c, pl.ds(0, n_expert - 1)], rs.at[BOX + c])

        @pl.loop(0, hid // tile)
        def _(n):
            at = pl.ds(pl.multiple_of(n * tile, tile), tile)
            pre = dot(inbox[c].reshape(slots, CHUNK), w_in[c * CHUNK : (c + 1) * CHUNK, at])
            pre_acc[:, at] = pre if c == 0 else pre_acc[:, at] + pre

    last = n_chunks - 1
    took(inbox.at[last, pl.ds(0, n_expert - 1)], rs.at[BOX + last])
    for half in range(HALVES):
        acc[...] = jnp.zeros_like(acc)
        mine = slice(half * rel_per, (half + 1) * rel_per)

        @pl.loop(0, hid // tile)
        def _(n):
            at = pl.ds(pl.multiple_of(n * tile, tile), tile)
            pre = dot(inbox[last, mine].reshape(m_rows, CHUNK), w_in[last * CHUNK : (last + 1) * CHUNK, at])
            pre += pre_acc[half * m_rows : (half + 1) * m_rows, at]
            hidden, grad = silu_and_slope(pre)
            slope[half, :, at] = grad.astype(BF16)
            acc[...] += dot(hidden.astype(BF16), w_out[at, :])

        made[mine] = acc[...].astype(BF16).reshape(rel_per, cap, eout)
        for i in others:
            if i // rel_per == half:
                remote(made.at[i], returned.at[e], BACK, BACK, t, rel_expert(i)).start()

    sent.append((made.at[pl.ds(0, n_expert - 1)], BACK))
    returned[e] = made[me]
    tin_copy.wait()
    took(returned.at[pl.ds(0, n_expert - 1)], rs.at[BACK])

    answers = returned[...].reshape(slots, eout)
    combined = (gate0 * dot(place[0], answers) + gate1 * dot(place[1], answers)).astype(BF16)
    comb[0] = combined
    per_half = tasks // 2
    for k in range(tasks):
        pre = dot(combined, tin[:, k * tw : (k + 1) * tw])
        units, unit_slope = silu_and_slope(pre)
        out_row = tout[k : k + 1, :]
        logit = jnp.sum(units * out_row, axis=1, keepdims=True)
        dlogit = (jax.nn.sigmoid(logit) - columns[:, 8 + k : 9 + k]) / tasks
        gto_out[0, k : k + 1, :] = jnp.sum(dlogit * units, axis=0, keepdims=True)
        grad = (dlogit * out_row * unit_slope).astype(BF16)
        dtow[k // per_half, :, (k % per_half) * tw : (k % per_half + 1) * tw] = grad
    to_sibling(comb.at[0], comb.at[1], COMB)
    to_sibling(dtow.at[sib], dtow_own.at[1], DTOW)
    dcomb = sum(dot_nt(dtow[h], tin[:, h * per_half * tw : (h + 1) * per_half * tw]) for h in range(2))
    dent = jnp.concatenate([(gate0 * dcomb).astype(BF16), (gate1 * dcomb).astype(BF16)], axis=0)
    dout[...] = dot(place_both_t[...], dent).astype(BF16).reshape(n_expert, cap, eout)
    for i in reversed(others):
        at = rel_back(i)
        to = rel_expert(i)
        remote(dout.at[to], din.at[at], DBOX, DBOX + at // rel_per, t, to).start()
    sent.append((dout.at[pl.ds(0, n_expert - 1)], DBOX))
    din[me] = dout[e]

    fan_a(lambda to: gto_out.at[0], gto_a.at[a], GTO_A, gto_a.at[pl.ds(0, side - 1)])
    gto_a[a] = gto_out[0]
    dtow_own[0] = dtow[core]
    comb_t[:, 0:batch] = comb[0].astype(F32).T.astype(BF16)
    took(comb.at[1], rs.at[COMB])
    took(dtow_own.at[1], rs.at[DTOW])
    comb_t[:, batch : 2 * batch] = comb[1].astype(F32).T.astype(BF16)
    t_rows = eout // n_table
    t_cols = tasks * tw // 2
    big = side * t_rows

    @pl.loop(0, side)
    def _(i):
        block = dot(comb_t[pl.ds(pl.multiple_of(i * big, big), big), :], dtow_own[...].reshape(2 * batch, t_cols))
        tower_a_out[i] = block.astype(BF16)

    fan_a(lambda to: tower_a_out.at[to], tower_a_in.at[a], TOW_A, tower_a_in.at[pl.ds(0, side - 1)])
    tower_a_in[a] = tower_a_out[a]

    n_wide = width // WIDE

    def token_grads(half, c):
        block = dot_nt(slope[half], w_in[c * WIDE : (c + 1) * WIDE, :])
        drows[c, half * rel_per : (half + 1) * rel_per] = block.astype(BF16).reshape(rel_per, cap, WIDE)
        for i in reversed(others):
            if i // rel_per == half:
                remote(drows.at[c, i], dback.at[c, e], DBACK + c, DBACK + c, t, rel_expert(i)).start()

    def tower_first():
        took(tower_a_in.at[pl.ds(0, side - 1)], rs.at[TOW_A])
        took(gto_a.at[pl.ds(0, side - 1)], rs.at[GTO_A])
        tower_b_out[...] = sum_of(tower_a_in, side).astype(BF16).reshape(side, t_rows, t_cols)
        fan_b(lambda to: tower_b_out.at[to], tower_b_in.at[b], TOW_B, tower_b_in.at[pl.ds(0, side - 1)])
        tower_b_in[b] = tower_b_out[b]
        gto_out[1] = sum_of(gto_a, side)
        fan_b(lambda to: gto_out.at[1], gto_b.at[b], GTO_B, gto_b.at[pl.ds(0, side - 1)])
        gto_b[b] = gto_out[1]

    for half in reversed(range(HALVES)):
        took(din.at[arrived(half)], rs.at[DBOX + half])
        mine = slice(half * rel_per, (half + 1) * rel_per)

        @pl.loop(0, hid // tile)
        def _(n):
            at = pl.ds(pl.multiple_of(n * tile, tile), tile)
            dhid = dot_nt(din[mine].reshape(m_rows, eout), w_out[at, :])
            slope[half, :, at] = (dhid * slope[half, :, at].astype(F32)).astype(BF16)

        if half == 0:
            tower_first()
        for c in range(n_wide):
            token_grads(half, c)

    for c in range(n_wide):
        dback[c, e] = drows[c, me]
        sent.append((drows.at[c, pl.ds(0, n_expert - 1)], DBACK + c))

    def pooled_grads(c):
        took(dback.at[c, pl.ds(0, n_expert - 1)], rs.at[DBACK + c])
        got = dot(place_sum[...], dback[c].reshape(slots, WIDE)).astype(BF16).astype(F32)
        for f in range(WIDE // LANES):
            dpooled_t[c, 0, :, f * batch : (f + 1) * batch] = got[:, f * LANES : (f + 1) * LANES].T.astype(BF16)
        to_sibling(dpooled_t.at[c, 0], dpooled_t.at[c, 1], DPOOL + c)

    def row_grads(c, s, at_a):
        parts = [
            counts[s, c * WIDE : (c + 1) * WIDE, pl.ds(pl.multiple_of((bb * side + at_a) * span, span), span)]
            for bb in range(side)
        ]
        return dot(dpooled_t[c, s], jnp.concatenate(parts, axis=1))

    def add_chunk(c, s):
        if s == 1:
            took(dpooled_t.at[c, 1], rs.at[DPOOL + c])
        for at_a in range(side):
            part = row_grads(c, s, at_a)
            grad_acc[at_a] = part if c == 0 and s == 0 else grad_acc[at_a] + part

    def gin_rows(at, n):
        return pl.ds(pl.multiple_of(at * t_rows, t_rows), n * t_rows)

    x_cols = t_cols // n_x
    x_at = pl.ds(pl.multiple_of(x * x_cols, x_cols), x_cols)
    my_rows, my_big = gin_rows(a * side + b, 1), gin_rows(a * side, side)
    from_b = gin.at[0, pl.ds(0, (side - 1) * t_rows), pl.ds(0, x_cols)]
    from_x = gin.at[0, pl.ds(0, side * t_rows), pl.ds(0, (n_x - 1) * x_cols)]

    def tower_second():
        took(tower_b_in.at[pl.ds(0, side - 1)], rs.at[TOW_B])
        took(gto_b.at[pl.ds(0, side - 1)], rs.at[GTO_B])
        total = sum_of(tower_b_in, side)
        for k in range(n_x):
            tower_x_out[k] = total[:, k * x_cols : (k + 1) * x_cols].astype(BF16)
        fan_x(lambda to: tower_x_out.at[to], tower_x_in.at[x], TOW_X, tower_x_in.at[pl.ds(0, n_x - 1)])
        tower_x_in[x] = tower_x_out[x]
        gto_out[2] = sum_of(gto_b, side)
        for i in others:
            remote(gto_out.at[2], gto_e.at[e], GTO_E, GTO_E, t, rel_expert(i)).start()
        sent.append((gto_e.at[pl.ds(0, n_expert - 1)], GTO_E))
        gto_e[e] = gto_out[2]

    def tower_x():
        took(tower_x_in.at[pl.ds(0, n_x - 1)], rs.at[TOW_X])
        gin[core, my_rows, x_at] = sum_of(tower_x_in, n_x).astype(BF16)
        block = gin.at[core, my_rows, x_at]
        fan_b(lambda to: block, block, GIN_B, from_b)

    def gather_b():
        took(from_b, rs.at[GIN_B])
        block = gin.at[core, my_big, x_at]
        fan_x(lambda to: block, block, GIN_X, from_x)

    gin_outs = []

    def gin_out(half, at_a):
        at = gin_rows(at_a * side, side)
        copy = local(gin.at[half, at], gin_hbm.at[at, pl.ds(pl.multiple_of(half * t_cols, t_cols), t_cols)], 9 + len(gin_outs))
        copy.start()
        gin_outs.append(copy)

    def whole(i):
        at_a = lax.rem(a + i, side)
        block = gin.at[core, gin_rows(at_a * side, side)]
        to_sibling(block, block, GIN_S + i)
        gin_out(core, at_a)

    def gather_x():
        took(from_x, rs.at[GIN_X])
        block = gin.at[core, my_big]
        for i in range(1, side):
            to = lax.rem(a + i, side)
            remote(block, block, GIN_A + i, GIN_A + side - i, to * a_step + b * b_step, e).start()
            sent.append((block, GIN_A + i))
        whole(0)

    def gather_a(i):
        took(gin.at[0, my_big], rs.at[GIN_A + i])
        whole(i)

    def from_sibling(i):
        took(gin.at[0, my_big], rs.at[GIN_S + i])
        gin_out(sib, lax.rem(b + i, side))

    tower_second()
    last = n_wide - 1
    for c in range(n_wide):
        pooled_grads(c)
        if c > 0:
            add_chunk(c - 1, 1)
        add_chunk(c, 0)
    took(dpooled_t.at[last, 1], rs.at[DPOOL + last])
    tower_x()
    for i in range(1, side):
        to = lax.rem(a + i, side)
        ga_out[to] = (grad_acc[to] + row_grads(last, 1, to)).astype(BF16)
        remote(ga_out.at[to], ga_in.at[a], GRAD_A, GRAD_A, to * a_step + b * b_step, e).start()
    sent.append((ga_in.at[pl.ds(0, side - 1)], GRAD_A))
    ga_in[a] = (grad_acc[a] + row_grads(last, 1, a)).astype(BF16)

    gather_b()
    gather_x()
    took(ga_in.at[pl.ds(0, side - 1)], rs.at[GRAD_A])
    total = sum_of(ga_in, side)
    for k in range(side):
        gb_out[k] = total[:, k * span : (k + 1) * span].astype(BF16)
    fan_b(lambda to: gb_out.at[to], gb_in.at[b], GRAD_B, gb_in.at[pl.ds(0, side - 1)])
    gb_in[b] = gb_out[b]
    took(gto_e.at[pl.ds(0, n_expert - 1)], rs.at[GTO_E])
    gtout[...] = sum_of(gto_e, n_expert)
    gto_copy = local(gtout, gtout_hbm, 9 + 2 * side)
    gto_copy.start()
    took(gb_in.at[pl.ds(0, side - 1)], rs.at[GRAD_B])
    gx_out[...] = sum_of(gb_in, side).T.astype(BF16).reshape(n_x, per, LANES)
    fan_x(lambda to: gx_out.at[to], gx_in.at[x], GRAD_X, gx_in.at[pl.ds(0, n_x - 1)])
    gx_in[x] = gx_out[x]
    for i in range(1, side):
        gather_a(i)
    took(gx_in.at[pl.ds(0, n_x - 1)], rs.at[GRAD_X])
    grows[...] = sum_of(gx_in, n_x)
    grows_copy = local(grows, grows_hbm, 10 + 2 * side)
    grows_copy.start()
    for i in range(side):
        from_sibling(i)

    for ref, k in sent:
        took(ref, ss.at[k])
    for copy in gin_outs + [gto_copy, grows_copy]:
        copy.wait()


def finish(gin_hbm, grows_hbm, gto_hbm, gin_out, grows_out, gto_out, narrow, wide, sem_in, sem_out):
    n = sem_in.shape[0] - 2
    step = narrow.shape[0] // n
    pieces = [pl.ds(i * step, step) for i in range(n)]
    ins = [pltpu.make_async_copy(gin_hbm.at[p], narrow.at[p], sem_in.at[i]) for i, p in enumerate(pieces)]
    outs = [pltpu.make_async_copy(wide.at[p], gin_out.at[p], sem_out.at[i]) for i, p in enumerate(pieces)]
    small = [
        pltpu.make_async_copy(grows_hbm, grows_out, sem_in.at[n]),
        pltpu.make_async_copy(gto_hbm, gto_out, sem_in.at[n + 1]),
    ]
    for copy in ins + small:
        copy.start()
    for i, p in enumerate(pieces):
        ins[i].wait()
        wide[p] = narrow[p].astype(F32)
        outs[i].start()
    for copy in outs + small:
        copy.wait()


def per_device(emb_rows, row_ids, route_ids, route_gates, w_in, w_out, tower_in, tower_out, labels):
    n_table = lax.axis_size("table")
    n_expert = lax.axis_size("expert")
    n_x = n_expert // 2
    side = math.isqrt(n_table)
    samples, tables, bag = row_ids.shape
    cap = 3 * samples // n_expert
    row_dev, dim = emb_rows.shape
    width = tables * dim
    hid, eout = w_out.shape[1:]
    tasks, tw = tower_out.shape
    per = row_dev // n_expert
    span = n_x * per
    cols = n_table * span
    slots = n_expert * cap
    n_chunks = width // CHUNK
    m_rows = slots // HALVES
    t_rows = eout // n_table
    t_cols = tasks * tw // 2
    x_cols = t_cols // n_x
    n_wide = width // WIDE
    hbm = pl.BlockSpec(memory_space=pl.ANY)
    dma = pltpu.SemaphoreType.DMA
    scratch = [
        pltpu.VMEM((width, hid), BF16),
        pltpu.VMEM((hid, eout), BF16),
        pltpu.VMEM((eout, tasks * tw), BF16),
        pltpu.VMEM((2, tables * bag, samples), jnp.int32),
        pltpu.VMEM((2, samples), jnp.int32),
        pltpu.VMEM((LANES, samples), F32),
        pltpu.VMEM((tasks, tw), F32),
        pltpu.VMEM((per, dim), F32),
        pltpu.VMEM((tasks, tw), F32),
        pltpu.VMEM((2, width, cols), BF16),
        pltpu.VMEM((side, side, n_x, per, LANES), BF16),
        pltpu.VMEM((n_chunks, CHUNK, LANES), F32),
        pltpu.VMEM((n_chunks, CHUNK, LANES), F32),
        pltpu.VMEM((n_chunks, CHUNK, LANES), F32),
        pltpu.VMEM((2, samples, slots), BF16),
        pltpu.VMEM((samples, slots), BF16),
        pltpu.VMEM((slots, samples), BF16),
        pltpu.VMEM((slots, 2 * samples), BF16),
        pltpu.VMEM((n_chunks, n_expert, cap, CHUNK), BF16),
        pltpu.VMEM((n_chunks, n_expert, cap, CHUNK), BF16),
        pltpu.VMEM((m_rows, eout), F32),
        pltpu.VMEM((slots, hid), F32),
        pltpu.VMEM((HALVES, m_rows, hid), BF16),
        pltpu.VMEM((n_expert, cap, eout), BF16),
        pltpu.VMEM((n_expert, cap, eout), BF16),
        pltpu.VMEM((2, samples, eout), BF16),
        pltpu.VMEM((2, samples, t_cols), BF16),
        pltpu.VMEM((2, samples, t_cols), BF16),
        pltpu.VMEM((eout, 2 * samples), BF16),
        pltpu.VMEM((side, side * t_rows, t_cols), BF16),
        pltpu.VMEM((side, side * t_rows, t_cols), BF16),
        pltpu.VMEM((side, t_rows, t_cols), BF16),
        pltpu.VMEM((side, t_rows, t_cols), BF16),
        pltpu.VMEM((n_x, t_rows, x_cols), BF16),
        pltpu.VMEM((n_x, t_rows, x_cols), BF16),
        pltpu.VMEM((2, eout, t_cols), BF16),
        pltpu.VMEM((3, tasks, tw), F32),
        pltpu.VMEM((side, tasks, tw), F32),
        pltpu.VMEM((side, tasks, tw), F32),
        pltpu.VMEM((n_expert, tasks, tw), F32),
        pltpu.VMEM((n_expert, cap, eout), BF16),
        pltpu.VMEM((n_expert, cap, eout), BF16),
        pltpu.VMEM((n_wide, n_expert, cap, WIDE), BF16),
        pltpu.VMEM((n_wide, n_expert, cap, WIDE), BF16),
        pltpu.VMEM((n_wide, 2, LANES, WIDE), BF16),
        pltpu.VMEM((side, LANES, side * span), F32),
        pltpu.VMEM((side, LANES, side * span), BF16),
        pltpu.VMEM((side, LANES, side * span), BF16),
        pltpu.VMEM((side, LANES, span), BF16),
        pltpu.VMEM((side, LANES, span), BF16),
        pltpu.VMEM((n_x, per, LANES), BF16),
        pltpu.VMEM((n_x, per, LANES), BF16),
        dma((11 + 2 * side,)),
        dma((N_SEMS,)),
        dma((N_SEMS,)),
    ]
    grows, gin, gtout = pl.pallas_call(
        functools.partial(kernel, n_table, n_expert),
        out_shape=(
            jax.ShapeDtypeStruct((per, dim), F32),
            jax.ShapeDtypeStruct((eout, tasks * tw), BF16),
            jax.ShapeDtypeStruct((tasks, tw), F32),
        ),
        in_specs=[hbm] * 9,
        out_specs=(hbm,) * 3,
        scratch_shapes=scratch,
        compiler_params=pltpu.CompilerParams(
            collective_id=0, has_side_effects=True, vmem_limit_bytes=VMEM_LIMIT
        ),
    )(
        jnp.transpose(row_ids, (1, 2, 0)).reshape(tables * bag, samples),
        emb_rows.reshape(n_x, 2, per, dim),
        route_ids.T,
        route_gates.T,
        labels.T,
        tower_out,
        w_in[0],
        w_out[0],
        tower_in,
    )
    gin, grows, gtout = pl.pallas_call(
        finish,
        out_shape=(
            jax.ShapeDtypeStruct((eout, tasks * tw), F32),
            jax.ShapeDtypeStruct((per, dim), F32),
            jax.ShapeDtypeStruct((tasks, tw), F32),
        ),
        in_specs=[hbm] * 3,
        out_specs=(hbm,) * 3,
        scratch_shapes=[
            pltpu.VMEM((eout, tasks * tw), BF16),
            pltpu.VMEM((eout, tasks * tw), F32),
            dma((10,)),
            dma((8,)),
        ],
    )(gin, grows, gtout)
    return grows, gin, gtout


VMEM_LIMIT = 63 * 1024 * 1024


def solution(mesh):
    return jax.shard_map(
        per_device,
        mesh=mesh,
        in_specs=(
            P("table", None),
            P(("table", "expert"), None, None),
            P(("table", "expert"), None),
            P(("table", "expert"), None),
            P("expert", None, None),
            P("expert", None, None),
            P(),
            P(),
            P(("table", "expert"), None),
        ),
        out_specs=(P(("table", "expert"), None), P(), P()),
        check_vma=False,
    )
```

```python
import functools
import math

import jax
import jax.numpy as jnp
from jax import lax
from jax.experimental import pallas as pl
from jax.experimental.pallas import tpu as pltpu
from jax.sharding import PartitionSpec as P

MESH = pl.DeviceIdType.MESH
F32 = jnp.float32
BF16 = jnp.bfloat16
LANES = 128
HALVES = 2
CHUNK = 256
WIDE = 512
TILE = 4096


IDS, EMB_A, EMB_B, COMB, DTOW, GTO_A, GTO_B, GTO_E = range(8)
TOW_A, TOW_B, TOW_X, GIN_B, GIN_X = range(8, 13)
BACK, GRAD_A, GRAD_B, GRAD_X = range(15, 19)
EMB_B0 = 19
DBOX = 20
PART = 24
DBACK = 28
DPOOL = 32
BOX = 36
GIN_A = 40
GIN_S = 44
N_SEMS = 48


def dot(a, b):
    return lax.dot_general(a, b, (((1,), (0,)), ((), ())), preferred_element_type=F32)


def dot_nt(a, b):
    return lax.dot_general(a, b, (((1,), (1,)), ((), ())), preferred_element_type=F32)


def silu_and_slope(pre):
    sig = 0.5 * jnp.tanh(0.5 * pre) + 0.5
    out = pre * sig
    return out, sig + out * (1.0 - sig)


def kernel(
    n_table,
    n_expert,
    ids_hbm,
    emb_hbm,
    route_hbm,
    gate_hbm,
    labels_hbm,
    tout_hbm,
    w_in_hbm,
    w_out_hbm,
    tin_hbm,
    grows_hbm,
    gin_hbm,
    gtout_hbm,
    w_in,
    w_out,
    tin,
    ids,
    route,
    narrow,
    tout,
    grows,
    gtout,
    counts,
    rows,
    part_out,
    part_own,
    part_in,
    place,
    place_sum,
    place_t,
    place_both_t,
    outbox,
    inbox,
    acc,
    pre_acc,
    slope,
    made,
    returned,
    comb,
    dtow,
    dtow_own,
    comb_t,
    tower_a_out,
    tower_a_in,
    tower_b_out,
    tower_b_in,
    tower_x_out,
    tower_x_in,
    gin,
    gto_out,
    gto_a,
    gto_b,
    gto_e,
    dout,
    din,
    drows,
    dback,
    dpooled_t,
    grad_acc,
    ga_out,
    ga_in,
    gb_out,
    gb_in,
    gx_out,
    gx_in,
    local_sem,
    ss,
    rs,
):
    t = lax.axis_index("table")
    e = lax.axis_index("expert")
    n_x = n_expert // 2
    side = math.isqrt(n_table)
    x = e // 2
    core = e % 2
    sib = 1 - core
    first = core == 0
    a = jnp.where(first, t // side, t % side)
    b = jnp.where(first, t % side, t // side)
    a_step = jnp.where(first, side, 1)
    b_step = jnp.where(first, 1, side)
    lookups, batch = ids.shape[1:]
    n_chunks = outbox.shape[0]
    width = n_chunks * CHUNK
    n_feat = width // LANES
    bag = lookups // n_feat
    cap = inbox.shape[2]
    slots = n_expert * cap
    hid = w_in.shape[1]
    eout = w_out.shape[1]
    tasks, tw = tout.shape
    per = rows.shape[3]
    span = n_x * per
    cols = n_table * span
    rel_per = n_expert // HALVES
    m_rows = rel_per * cap
    per_chunk = CHUNK // LANES

    far = n_x // 2
    rels = [(far, 0), (far, 1)]
    rels += [(d, 0) for d in range(1, n_x) if d != far]
    rels += [(0, 0), (0, 1)]
    rels += [(d, 1) for d in range(1, n_x) if d != far]
    me = rels.index((0, 0))
    others = [i for i in range(n_expert) if i != me]

    def rel_expert(i):
        d, c = rels[i]
        return lax.rem(x + d, n_x) * 2 + lax.rem(core + c, 2)

    def rel_back(i):
        d, c = rels[i]
        return rels.index(((n_x - d) % n_x, c))

    def remote(src, dst, k_send, k_recv, to_t, to_e):
        return pltpu.make_async_remote_copy(
            src_ref=src, dst_ref=dst, send_sem=ss.at[k_send], recv_sem=rs.at[k_recv],
            device_id=(to_t, to_e), device_id_type=MESH,
        )

    def took(ref, sem):
        pltpu.make_async_copy(ref, ref, sem).wait()

    sent = []

    def to_sibling(src, dst, k):
        remote(src, dst, k, k, t, x * 2 + sib).start()
        sent.append((src, k))

    def fan_a(src, dst, k, total):
        for i in range(1, side):
            to = lax.rem(a + i, side)
            remote(src(to), dst, k, k, to * a_step + b * b_step, e).start()
        sent.append((total, k))

    def fan_b(src, dst, k, total):
        for i in range(1, side):
            to = lax.rem(b + i, side)
            remote(src(to), dst, k, k, a * a_step + to * b_step, e).start()
        sent.append((total, k))

    def fan_x(src, dst, k, total):
        for i in range(1, n_x):
            to = lax.rem(x + i, n_x)
            remote(src(to), dst, k, k, t, to * 2 + core).start()
        sent.append((total, k))

    def sum_of(ref, n):
        total = ref[0].astype(F32)
        for i in range(1, n):
            total += ref[i].astype(F32)
        return total

    barrier = pltpu.get_barrier_semaphore()
    for i in range(1, side):
        for to_t in (lax.rem(a + i, side) * a_step + b * b_step, a * a_step + lax.rem(b + i, side) * b_step):
            pl.semaphore_signal(barrier, inc=1, device_id=(to_t, e), device_id_type=MESH)
    for i in others:
        pl.semaphore_signal(barrier, inc=1, device_id=(t, rel_expert(i)), device_id_type=MESH)

    def local(src, dst, k):
        return pltpu.make_async_copy(src, dst, local_sem.at[k])

    ids_copy = local(ids_hbm, ids.at[0], 0)
    emb_copy = local(emb_hbm.at[:, core], rows.at[b, a], 1)
    small = [
        local(route_hbm, route, 2),
        local(gate_hbm, narrow.at[pl.ds(0, 2)], 3),
        local(labels_hbm, narrow.at[pl.ds(8, tasks)], 4),
        local(tout_hbm, tout, 5),
    ]
    w_in_copy = local(w_in_hbm, w_in, 6)
    w_out_copy = local(w_out_hbm, w_out, 7)
    tin_copy = local(tin_hbm, tin, 8)
    for copy in [emb_copy, ids_copy] + small:
        copy.start()
    emb_copy.wait()
    ids_copy.wait()
    pl.semaphore_wait(barrier, 2 * (side - 1) + n_expert - 1)

    fan_a(lambda to: rows.at[b, a], rows.at[b, a], EMB_A, rows.at[0, pl.ds(0, side - 1)])
    fan_b(lambda to: rows.at[b, a], rows.at[b, a], EMB_B0, rows.at[0, pl.ds(0, side - 1)])
    to_sibling(ids.at[0], ids.at[1], IDS)
    w_in_copy.start()
    w_out_copy.start()
    tin_copy.start()

    for copy in small:
        copy.wait()
    columns = narrow[...].T
    named_by = jnp.concatenate([route[...].astype(F32), jnp.zeros((LANES - 2, batch), F32)], axis=0).T.astype(jnp.int32)
    lane = lax.broadcasted_iota(jnp.int32, (batch, LANES), 1)
    slot_lane = lax.broadcasted_iota(jnp.int32, (batch, slots), 1)
    r0, r1 = named_by[:, 0:1], named_by[:, 1:2]
    gate0, gate1 = columns[:, 0:1], columns[:, 1:2]
    named0, named1 = lane == r0, lane == r1
    named = jnp.where(named0 | named1, 1.0, 0.0).astype(BF16)
    earlier = jnp.where(
        lax.broadcasted_iota(jnp.int32, (batch, batch), 1) < lax.broadcasted_iota(jnp.int32, (batch, batch), 0),
        1.0, 0.0,
    ).astype(BF16)
    before = dot(earlier, named)
    placed = []
    for j, (r, hit) in enumerate(((r0, named0), (r1, named1))):
        pos = jnp.sum(jnp.where(hit, before, 0.0), axis=1, keepdims=True).astype(jnp.int32)
        placed.append(jnp.where(slot_lane == r * cap + pos, 1.0, 0.0))
        place[j] = placed[j].astype(BF16)
        place_both_t[:, j * batch : (j + 1) * batch] = placed[j].T.astype(BF16)
    both = placed[0] + placed[1]
    place_sum[...] = both.astype(BF16)
    place_t[...] = both.T.astype(BF16)

    def code_of(s):
        own = ids[s]
        shard = own // (n_x * 2 * per)
        near = lax.rem(own // (2 * per), n_x) * per + lax.rem(own, per)
        at_a = jnp.where(first, shard // side, lax.rem(shard, side))
        at_b = jnp.where(first, lax.rem(shard, side), shard // side)
        code = jnp.where(lax.rem(own // per, 2) == core, (at_b * side + at_a) * span + near, -1)
        flat = jnp.concatenate([code.astype(F32), jnp.zeros((LANES - lookups, batch), F32)], axis=0)
        return flat.T.astype(jnp.int32)

    def build_counts(s, code, features):
        for f in features:
            words = [jnp.zeros((batch, LANES), jnp.int32) for _ in range(-(-cols // (8 * LANES)))]
            for k in range(bag):
                c = f * bag + k
                gap = code[:, c : c + 1] - lane
                high = gap >> 7
                one = jnp.where(jnp.bitwise_and(gap, LANES - 1) == 0, 1 << (jnp.bitwise_and(high, 7) * 4), 0)
                which = high >> 3
                for w in range(len(words)):
                    words[w] = words[w] + jnp.where(which == w, one, 0)
            for h in range(cols // LANES):
                count = jnp.bitwise_and(words[h // 8] >> (4 * (h % 8)), 15)
                counts[s, f * batch : (f + 1) * batch, h * LANES : (h + 1) * LANES] = count.astype(F32).astype(BF16)

    build_counts(0, code_of(0), range(n_feat))
    took(rows.at[0, pl.ds(0, side - 1)], rs.at[EMB_A])
    for i in range(1, side):
        block = rows.at[b, lax.rem(a + i, side)]
        for j in range(1, side):
            to = lax.rem(b + j, side)
            remote(block, block, EMB_B, EMB_B, a * a_step + to * b_step, e).start()
    sent.append((rows.at[pl.ds(0, side - 1), pl.ds(0, side - 1)], EMB_B))
    took(ids.at[1], rs.at[IDS])
    build_counts(1, code_of(1), range(n_feat))

    part_cols = side * span

    def partial(s, c, at_b):
        at = pl.ds(pl.multiple_of(at_b * part_cols, part_cols), part_cols)
        return dot(counts[s, c * CHUNK : (c + 1) * CHUNK, at], rows[at_b].reshape(part_cols, LANES))

    for c in range(n_chunks):
        part_out[c] = partial(1, c, b)
        part_own[c] = partial(0, c, b)
    took(rows.at[0, pl.ds(0, side - 1)], rs.at[EMB_B0])
    took(rows.at[pl.ds(0, side - 1), pl.ds(0, side - 1)], rs.at[EMB_B])

    def all_parts(s, c, total):
        for i in range(1, side):
            total += partial(s, c, lax.rem(b + i, side))
        return total

    def swap_partial(c):
        part_out[c] = all_parts(1, c, part_out[c])
        to_sibling(part_out.at[c], part_in.at[c], PART + c)

    swap_partial(0)
    for c in range(n_chunks):
        mine = all_parts(0, c, part_own[c])
        if c + 1 < n_chunks:
            swap_partial(c + 1)
        took(part_in.at[c], rs.at[PART + c])
        pooled = (mine + part_in[c]).astype(BF16)
        tokens = jnp.concatenate([pooled[f * batch : (f + 1) * batch] for f in range(per_chunk)], axis=1)
        outbox[c] = dot(place_t[...], tokens).astype(BF16).reshape(n_expert, cap, CHUNK)
        for i in others:
            to = rel_expert(i)
            remote(outbox.at[c, to], inbox.at[c, rel_back(i)], BOX + c, BOX + c, t, to).start()
        sent.append((outbox.at[c, pl.ds(0, n_expert - 1)], BOX + c))
        inbox[c, me] = outbox[c, e]

    w_in_copy.wait()
    w_out_copy.wait()

    def arrived(half):
        return pl.ds(half * rel_per, rel_per - (me // rel_per == half))

    tile = min(TILE, hid)

    for c in range(n_chunks - 1):
        took(inbox.at[c, pl.ds(0, n_expert - 1)], rs.at[BOX + c])

        @pl.loop(0, hid // tile)
        def _(n):
            at = pl.ds(pl.multiple_of(n * tile, tile), tile)
            pre = dot(inbox[c].reshape(slots, CHUNK), w_in[c * CHUNK : (c + 1) * CHUNK, at])
            pre_acc[:, at] = pre if c == 0 else pre_acc[:, at] + pre

    last = n_chunks - 1
    took(inbox.at[last, pl.ds(0, n_expert - 1)], rs.at[BOX + last])
    for half in range(HALVES):
        acc[...] = jnp.zeros_like(acc)
        mine = slice(half * rel_per, (half + 1) * rel_per)

        @pl.loop(0, hid // tile)
        def _(n):
            at = pl.ds(pl.multiple_of(n * tile, tile), tile)
            pre = dot(inbox[last, mine].reshape(m_rows, CHUNK), w_in[last * CHUNK : (last + 1) * CHUNK, at])
            pre += pre_acc[half * m_rows : (half + 1) * m_rows, at]
            hidden, grad = silu_and_slope(pre)
            slope[half, :, at] = grad.astype(BF16)
            acc[...] += dot(hidden.astype(BF16), w_out[at, :])

        made[mine] = acc[...].astype(BF16).reshape(rel_per, cap, eout)
        for i in others:
            if i // rel_per == half:
                remote(made.at[i], returned.at[e], BACK, BACK, t, rel_expert(i)).start()

    sent.append((made.at[pl.ds(0, n_expert - 1)], BACK))
    returned[e] = made[me]
    tin_copy.wait()
    took(returned.at[pl.ds(0, n_expert - 1)], rs.at[BACK])

    answers = returned[...].reshape(slots, eout)
    combined = (gate0 * dot(place[0], answers) + gate1 * dot(place[1], answers)).astype(BF16)
    comb[0] = combined
    per_half = tasks // 2
    for k in range(tasks):
        pre = dot(combined, tin[:, k * tw : (k + 1) * tw])
        units, unit_slope = silu_and_slope(pre)
        out_row = tout[k : k + 1, :]
        logit = jnp.sum(units * out_row, axis=1, keepdims=True)
        dlogit = (jax.nn.sigmoid(logit) - columns[:, 8 + k : 9 + k]) / tasks
        gto_out[0, k : k + 1, :] = jnp.sum(dlogit * units, axis=0, keepdims=True)
        grad = (dlogit * out_row * unit_slope).astype(BF16)
        dtow[k // per_half, :, (k % per_half) * tw : (k % per_half + 1) * tw] = grad
    to_sibling(comb.at[0], comb.at[1], COMB)
    to_sibling(dtow.at[sib], dtow_own.at[1], DTOW)
    dcomb = sum(dot_nt(dtow[h], tin[:, h * per_half * tw : (h + 1) * per_half * tw]) for h in range(2))
    dent = jnp.concatenate([(gate0 * dcomb).astype(BF16), (gate1 * dcomb).astype(BF16)], axis=0)
    dout[...] = dot(place_both_t[...], dent).astype(BF16).reshape(n_expert, cap, eout)
    for i in others:
        at = rel_back(i)
        to = rel_expert(i)
        remote(dout.at[to], din.at[at], DBOX, DBOX + at // rel_per, t, to).start()
    sent.append((dout.at[pl.ds(0, n_expert - 1)], DBOX))
    din[me] = dout[e]

    fan_a(lambda to: gto_out.at[0], gto_a.at[a], GTO_A, gto_a.at[pl.ds(0, side - 1)])
    gto_a[a] = gto_out[0]
    dtow_own[0] = dtow[core]
    comb_t[:, 0:batch] = comb[0].astype(F32).T.astype(BF16)
    took(comb.at[1], rs.at[COMB])
    took(dtow_own.at[1], rs.at[DTOW])
    comb_t[:, batch : 2 * batch] = comb[1].astype(F32).T.astype(BF16)
    t_rows = eout // n_table
    t_cols = tasks * tw // 2
    big = side * t_rows

    @pl.loop(0, side)
    def _(i):
        block = dot(comb_t[pl.ds(pl.multiple_of(i * big, big), big), :], dtow_own[...].reshape(2 * batch, t_cols))
        tower_a_out[i] = block.astype(BF16)

    fan_a(lambda to: tower_a_out.at[to], tower_a_in.at[a], TOW_A, tower_a_in.at[pl.ds(0, side - 1)])
    tower_a_in[a] = tower_a_out[a]

    n_wide = width // WIDE

    def token_grads(half, c):
        block = dot_nt(slope[half], w_in[c * WIDE : (c + 1) * WIDE, :])
        drows[c, half * rel_per : (half + 1) * rel_per] = block.astype(BF16).reshape(rel_per, cap, WIDE)
        for i in others:
            if i // rel_per == half:
                remote(drows.at[c, i], dback.at[c, e], DBACK + c, DBACK + c, t, rel_expert(i)).start()

    def tower_first():
        took(tower_a_in.at[pl.ds(0, side - 1)], rs.at[TOW_A])
        took(gto_a.at[pl.ds(0, side - 1)], rs.at[GTO_A])
        tower_b_out[...] = sum_of(tower_a_in, side).astype(BF16).reshape(side, t_rows, t_cols)
        fan_b(lambda to: tower_b_out.at[to], tower_b_in.at[b], TOW_B, tower_b_in.at[pl.ds(0, side - 1)])
        tower_b_in[b] = tower_b_out[b]
        gto_out[1] = sum_of(gto_a, side)
        fan_b(lambda to: gto_out.at[1], gto_b.at[b], GTO_B, gto_b.at[pl.ds(0, side - 1)])
        gto_b[b] = gto_out[1]

    for half in range(HALVES):
        took(din.at[arrived(half)], rs.at[DBOX + half])
        mine = slice(half * rel_per, (half + 1) * rel_per)

        @pl.loop(0, hid // tile)
        def _(n):
            at = pl.ds(pl.multiple_of(n * tile, tile), tile)
            dhid = dot_nt(din[mine].reshape(m_rows, eout), w_out[at, :])
            slope[half, :, at] = (dhid * slope[half, :, at].astype(F32)).astype(BF16)

        if half == HALVES - 1:
            tower_first()
        for c in range(n_wide):
            token_grads(half, c)

    for c in range(n_wide):
        dback[c, e] = drows[c, me]
        sent.append((drows.at[c, pl.ds(0, n_expert - 1)], DBACK + c))

    def pooled_grads(c):
        took(dback.at[c, pl.ds(0, n_expert - 1)], rs.at[DBACK + c])
        got = dot(place_sum[...], dback[c].reshape(slots, WIDE)).astype(BF16).astype(F32)
        for f in range(WIDE // LANES):
            dpooled_t[c, 0, :, f * batch : (f + 1) * batch] = got[:, f * LANES : (f + 1) * LANES].T.astype(BF16)
        to_sibling(dpooled_t.at[c, 0], dpooled_t.at[c, 1], DPOOL + c)

    def row_grads(c, s, at_a):
        parts = [
            counts[s, c * WIDE : (c + 1) * WIDE, pl.ds(pl.multiple_of((bb * side + at_a) * span, span), span)]
            for bb in range(side)
        ]
        return dot(dpooled_t[c, s], jnp.concatenate(parts, axis=1))

    def add_chunk(c, s):
        if s == 1:
            took(dpooled_t.at[c, 1], rs.at[DPOOL + c])
        for at_a in range(side):
            part = row_grads(c, s, at_a)
            grad_acc[at_a] = part if c == 0 and s == 0 else grad_acc[at_a] + part

    def gin_rows(at, n):
        return pl.ds(pl.multiple_of(at * t_rows, t_rows), n * t_rows)

    x_cols = t_cols // n_x
    x_at = pl.ds(pl.multiple_of(x * x_cols, x_cols), x_cols)
    my_rows, my_big = gin_rows(a * side + b, 1), gin_rows(a * side, side)
    from_b = gin.at[0, pl.ds(0, (side - 1) * t_rows), pl.ds(0, x_cols)]
    from_x = gin.at[0, pl.ds(0, side * t_rows), pl.ds(0, (n_x - 1) * x_cols)]

    def tower_second():
        took(tower_b_in.at[pl.ds(0, side - 1)], rs.at[TOW_B])
        took(gto_b.at[pl.ds(0, side - 1)], rs.at[GTO_B])
        total = sum_of(tower_b_in, side)
        for k in range(n_x):
            tower_x_out[k] = total[:, k * x_cols : (k + 1) * x_cols].astype(BF16)
        fan_x(lambda to: tower_x_out.at[to], tower_x_in.at[x], TOW_X, tower_x_in.at[pl.ds(0, n_x - 1)])
        tower_x_in[x] = tower_x_out[x]
        gto_out[2] = sum_of(gto_b, side)
        for i in others:
            remote(gto_out.at[2], gto_e.at[e], GTO_E, GTO_E, t, rel_expert(i)).start()
        sent.append((gto_e.at[pl.ds(0, n_expert - 1)], GTO_E))
        gto_e[e] = gto_out[2]

    def tower_x():
        took(tower_x_in.at[pl.ds(0, n_x - 1)], rs.at[TOW_X])
        gin[core, my_rows, x_at] = sum_of(tower_x_in, n_x).astype(BF16)
        block = gin.at[core, my_rows, x_at]
        fan_b(lambda to: block, block, GIN_B, from_b)

    def gather_b():
        took(from_b, rs.at[GIN_B])
        block = gin.at[core, my_big, x_at]
        fan_x(lambda to: block, block, GIN_X, from_x)

    gin_outs = []

    def gin_out(half, at_a):
        at = gin_rows(at_a * side, side)
        copy = local(gin.at[half, at], gin_hbm.at[at, pl.ds(pl.multiple_of(half * t_cols, t_cols), t_cols)], 9 + len(gin_outs))
        copy.start()
        gin_outs.append(copy)

    def whole(i):
        at_a = lax.rem(a + i, side)
        block = gin.at[core, gin_rows(at_a * side, side)]
        to_sibling(block, block, GIN_S + i)
        gin_out(core, at_a)

    def gather_x():
        took(from_x, rs.at[GIN_X])
        block = gin.at[core, my_big]
        for i in range(1, side):
            to = lax.rem(a + i, side)
            remote(block, block, GIN_A + i, GIN_A + side - i, to * a_step + b * b_step, e).start()
            sent.append((block, GIN_A + i))
        whole(0)

    def gather_a(i):
        took(gin.at[0, my_big], rs.at[GIN_A + i])
        whole(i)

    def from_sibling(i):
        took(gin.at[0, my_big], rs.at[GIN_S + i])
        gin_out(sib, lax.rem(b + i, side))

    tower_second()
    last = n_wide - 1
    for c in range(n_wide):
        pooled_grads(c)
        if c > 0:
            add_chunk(c - 1, 1)
            tower_x()
        add_chunk(c, 0)
    took(dpooled_t.at[last, 1], rs.at[DPOOL + last])
    for i in range(1, side):
        to = lax.rem(a + i, side)
        ga_out[to] = (grad_acc[to] + row_grads(last, 1, to)).astype(BF16)
        remote(ga_out.at[to], ga_in.at[a], GRAD_A, GRAD_A, to * a_step + b * b_step, e).start()
    sent.append((ga_in.at[pl.ds(0, side - 1)], GRAD_A))
    ga_in[a] = (grad_acc[a] + row_grads(last, 1, a)).astype(BF16)

    gather_b()
    gather_x()
    took(ga_in.at[pl.ds(0, side - 1)], rs.at[GRAD_A])
    total = sum_of(ga_in, side)
    for k in range(side):
        gb_out[k] = total[:, k * span : (k + 1) * span].astype(BF16)
    fan_b(lambda to: gb_out.at[to], gb_in.at[b], GRAD_B, gb_in.at[pl.ds(0, side - 1)])
    gb_in[b] = gb_out[b]
    took(gto_e.at[pl.ds(0, n_expert - 1)], rs.at[GTO_E])
    gtout[...] = sum_of(gto_e, n_expert)
    gto_copy = local(gtout, gtout_hbm, 9 + 2 * side)
    gto_copy.start()
    took(gb_in.at[pl.ds(0, side - 1)], rs.at[GRAD_B])
    gx_out[...] = sum_of(gb_in, side).T.astype(BF16).reshape(n_x, per, LANES)
    fan_x(lambda to: gx_out.at[to], gx_in.at[x], GRAD_X, gx_in.at[pl.ds(0, n_x - 1)])
    gx_in[x] = gx_out[x]
    for i in range(1, side):
        gather_a(i)
    took(gx_in.at[pl.ds(0, n_x - 1)], rs.at[GRAD_X])
    grows[...] = sum_of(gx_in, n_x)
    grows_copy = local(grows, grows_hbm, 10 + 2 * side)
    grows_copy.start()
    for i in range(side):
        from_sibling(i)

    for ref, k in sent:
        took(ref, ss.at[k])
    for copy in gin_outs + [gto_copy, grows_copy]:
        copy.wait()


def finish(gin_hbm, grows_hbm, gto_hbm, gin_out, grows_out, gto_out, narrow, wide, sem_in, sem_out):
    n = sem_in.shape[0] - 2
    step = narrow.shape[0] // n
    pieces = [pl.ds(i * step, step) for i in range(n)]
    ins = [pltpu.make_async_copy(gin_hbm.at[p], narrow.at[p], sem_in.at[i]) for i, p in enumerate(pieces)]
    outs = [pltpu.make_async_copy(wide.at[p], gin_out.at[p], sem_out.at[i]) for i, p in enumerate(pieces)]
    small = [
        pltpu.make_async_copy(grows_hbm, grows_out, sem_in.at[n]),
        pltpu.make_async_copy(gto_hbm, gto_out, sem_in.at[n + 1]),
    ]
    for copy in ins + small:
        copy.start()
    for i, p in enumerate(pieces):
        ins[i].wait()
        wide[p] = narrow[p].astype(F32)
        outs[i].start()
    for copy in outs + small:
        copy.wait()


def per_device(emb_rows, row_ids, route_ids, route_gates, w_in, w_out, tower_in, tower_out, labels):
    n_table = lax.axis_size("table")
    n_expert = lax.axis_size("expert")
    n_x = n_expert // 2
    side = math.isqrt(n_table)
    samples, tables, bag = row_ids.shape
    cap = 3 * samples // n_expert
    row_dev, dim = emb_rows.shape
    width = tables * dim
    hid, eout = w_out.shape[1:]
    tasks, tw = tower_out.shape
    per = row_dev // n_expert
    span = n_x * per
    cols = n_table * span
    slots = n_expert * cap
    n_chunks = width // CHUNK
    m_rows = slots // HALVES
    t_rows = eout // n_table
    t_cols = tasks * tw // 2
    x_cols = t_cols // n_x
    n_wide = width // WIDE
    hbm = pl.BlockSpec(memory_space=pl.ANY)
    dma = pltpu.SemaphoreType.DMA
    scratch = [
        pltpu.VMEM((width, hid), BF16),
        pltpu.VMEM((hid, eout), BF16),
        pltpu.VMEM((eout, tasks * tw), BF16),
        pltpu.VMEM((2, tables * bag, samples), jnp.int32),
        pltpu.VMEM((2, samples), jnp.int32),
        pltpu.VMEM((LANES, samples), F32),
        pltpu.VMEM((tasks, tw), F32),
        pltpu.VMEM((per, dim), F32),
        pltpu.VMEM((tasks, tw), F32),
        pltpu.VMEM((2, width, cols), BF16),
        pltpu.VMEM((side, side, n_x, per, LANES), BF16),
        pltpu.VMEM((n_chunks, CHUNK, LANES), F32),
        pltpu.VMEM((n_chunks, CHUNK, LANES), F32),
        pltpu.VMEM((n_chunks, CHUNK, LANES), F32),
        pltpu.VMEM((2, samples, slots), BF16),
        pltpu.VMEM((samples, slots), BF16),
        pltpu.VMEM((slots, samples), BF16),
        pltpu.VMEM((slots, 2 * samples), BF16),
        pltpu.VMEM((n_chunks, n_expert, cap, CHUNK), BF16),
        pltpu.VMEM((n_chunks, n_expert, cap, CHUNK), BF16),
        pltpu.VMEM((m_rows, eout), F32),
        pltpu.VMEM((slots, hid), F32),
        pltpu.VMEM((HALVES, m_rows, hid), BF16),
        pltpu.VMEM((n_expert, cap, eout), BF16),
        pltpu.VMEM((n_expert, cap, eout), BF16),
        pltpu.VMEM((2, samples, eout), BF16),
        pltpu.VMEM((2, samples, t_cols), BF16),
        pltpu.VMEM((2, samples, t_cols), BF16),
        pltpu.VMEM((eout, 2 * samples), BF16),
        pltpu.VMEM((side, side * t_rows, t_cols), BF16),
        pltpu.VMEM((side, side * t_rows, t_cols), BF16),
        pltpu.VMEM((side, t_rows, t_cols), BF16),
        pltpu.VMEM((side, t_rows, t_cols), BF16),
        pltpu.VMEM((n_x, t_rows, x_cols), BF16),
        pltpu.VMEM((n_x, t_rows, x_cols), BF16),
        pltpu.VMEM((2, eout, t_cols), BF16),
        pltpu.VMEM((3, tasks, tw), F32),
        pltpu.VMEM((side, tasks, tw), F32),
        pltpu.VMEM((side, tasks, tw), F32),
        pltpu.VMEM((n_expert, tasks, tw), F32),
        pltpu.VMEM((n_expert, cap, eout), BF16),
        pltpu.VMEM((n_expert, cap, eout), BF16),
        pltpu.VMEM((n_wide, n_expert, cap, WIDE), BF16),
        pltpu.VMEM((n_wide, n_expert, cap, WIDE), BF16),
        pltpu.VMEM((n_wide, 2, LANES, WIDE), BF16),
        pltpu.VMEM((side, LANES, side * span), F32),
        pltpu.VMEM((side, LANES, side * span), BF16),
        pltpu.VMEM((side, LANES, side * span), BF16),
        pltpu.VMEM((side, LANES, span), BF16),
        pltpu.VMEM((side, LANES, span), BF16),
        pltpu.VMEM((n_x, per, LANES), BF16),
        pltpu.VMEM((n_x, per, LANES), BF16),
        dma((11 + 2 * side,)),
        dma((N_SEMS,)),
        dma((N_SEMS,)),
    ]
    grows, gin, gtout = pl.pallas_call(
        functools.partial(kernel, n_table, n_expert),
        out_shape=(
            jax.ShapeDtypeStruct((per, dim), F32),
            jax.ShapeDtypeStruct((eout, tasks * tw), BF16),
            jax.ShapeDtypeStruct((tasks, tw), F32),
        ),
        in_specs=[hbm] * 9,
        out_specs=(hbm,) * 3,
        scratch_shapes=scratch,
        compiler_params=pltpu.CompilerParams(
            collective_id=0, has_side_effects=True, vmem_limit_bytes=VMEM_LIMIT
        ),
    )(
        jnp.transpose(row_ids, (1, 2, 0)).reshape(tables * bag, samples),
        emb_rows.reshape(n_x, 2, per, dim),
        route_ids.T,
        route_gates.T,
        labels.T,
        tower_out,
        w_in[0],
        w_out[0],
        tower_in,
    )
    gin, grows, gtout = pl.pallas_call(
        finish,
        out_shape=(
            jax.ShapeDtypeStruct((eout, tasks * tw), F32),
            jax.ShapeDtypeStruct((per, dim), F32),
            jax.ShapeDtypeStruct((tasks, tw), F32),
        ),
        in_specs=[hbm] * 3,
        out_specs=(hbm,) * 3,
        scratch_shapes=[
            pltpu.VMEM((eout, tasks * tw), BF16),
            pltpu.VMEM((eout, tasks * tw), F32),
            dma((10,)),
            dma((8,)),
        ],
    )(gin, grows, gtout)
    return grows, gin, gtout


VMEM_LIMIT = 63 * 1024 * 1024


def solution(mesh):
    return jax.shard_map(
        per_device,
        mesh=mesh,
        in_specs=(
            P("table", None),
            P(("table", "expert"), None, None),
            P(("table", "expert"), None),
            P(("table", "expert"), None),
            P("expert", None, None),
            P("expert", None, None),
            P(),
            P(),
            P(("table", "expert"), None),
        ),
        out_specs=(P(("table", "expert"), None), P(), P()),
        check_vma=False,
    )
```

```python
import functools
import math

import jax
import jax.numpy as jnp
from jax import lax
from jax.experimental import pallas as pl
from jax.experimental.pallas import tpu as pltpu
from jax.sharding import PartitionSpec as P

MESH = pl.DeviceIdType.MESH
F32 = jnp.float32
BF16 = jnp.bfloat16
LANES = 128
HALVES = 2
CHUNK = 256
WIDE = 512
TILE = 4096


IDS, EMB_A, EMB_B, COMB, DTOW, GTO_A, GTO_B, GTO_E = range(8)
TOW_A, TOW_B, TOW_X, GIN_B, GIN_X = range(8, 13)
BACK, GRAD_A, GRAD_B, GRAD_X = range(15, 19)
EMB_B0 = 19
DBOX = 20
PART = 24
DBACK = 28
DPOOL = 32
BOX = 36
GIN_A = 40
GIN_S = 44
GIN_A2, GIN_X2, GIN_S2 = 48, 49, 50
N_SEMS = 51


def dot(a, b):
    return lax.dot_general(a, b, (((1,), (0,)), ((), ())), preferred_element_type=F32)


def dot_nt(a, b):
    return lax.dot_general(a, b, (((1,), (1,)), ((), ())), preferred_element_type=F32)


def silu_and_slope(pre):
    sig = 0.5 * jnp.tanh(0.5 * pre) + 0.5
    out = pre * sig
    return out, sig + out * (1.0 - sig)


def kernel(
    n_table,
    n_expert,
    ids_hbm,
    emb_hbm,
    route_hbm,
    gate_hbm,
    labels_hbm,
    tout_hbm,
    w_in_hbm,
    w_out_hbm,
    tin_hbm,
    grows_hbm,
    gin_hbm,
    gtout_hbm,
    w_in,
    w_out,
    tin,
    ids,
    route,
    narrow,
    tout,
    grows,
    gtout,
    counts,
    rows,
    part_out,
    part_own,
    part_in,
    place,
    place_sum,
    place_t,
    place_both_t,
    outbox,
    inbox,
    acc,
    pre_acc,
    slope,
    made,
    returned,
    comb,
    dtow,
    dtow_own,
    comb_t,
    tower_a_out,
    tower_a_in,
    tower_b_out,
    tower_b_in,
    tower_x_out,
    tower_x_in,
    gin,
    gto_out,
    gto_a,
    gto_b,
    gto_e,
    dout,
    din,
    drows,
    dback,
    dpooled_t,
    grad_acc,
    ga_out,
    ga_in,
    gb_out,
    gb_in,
    gx_out,
    gx_in,
    local_sem,
    ss,
    rs,
):
    t = lax.axis_index("table")
    e = lax.axis_index("expert")
    n_x = n_expert // 2
    side = math.isqrt(n_table)
    x = e // 2
    core = e % 2
    sib = 1 - core
    first = core == 0
    a = jnp.where(first, t // side, t % side)
    b = jnp.where(first, t % side, t // side)
    a_step = jnp.where(first, side, 1)
    b_step = jnp.where(first, 1, side)
    lookups, batch = ids.shape[1:]
    n_chunks = outbox.shape[0]
    width = n_chunks * CHUNK
    n_feat = width // LANES
    bag = lookups // n_feat
    cap = inbox.shape[2]
    slots = n_expert * cap
    hid = w_in.shape[1]
    eout = w_out.shape[1]
    tasks, tw = tout.shape
    per = rows.shape[3]
    span = n_x * per
    cols = n_table * span
    rel_per = n_expert // HALVES
    m_rows = rel_per * cap
    per_chunk = CHUNK // LANES

    far = n_x // 2
    rels = [(far, 0), (far, 1)]
    rels += [(d, 0) for d in range(1, n_x) if d != far]
    rels += [(0, 0), (0, 1)]
    rels += [(d, 1) for d in range(1, n_x) if d != far]
    me = rels.index((0, 0))
    others = [i for i in range(n_expert) if i != me]

    def rel_expert(i):
        d, c = rels[i]
        return lax.rem(x + d, n_x) * 2 + lax.rem(core + c, 2)

    def rel_back(i):
        d, c = rels[i]
        return rels.index(((n_x - d) % n_x, c))

    def remote(src, dst, k_send, k_recv, to_t, to_e):
        return pltpu.make_async_remote_copy(
            src_ref=src, dst_ref=dst, send_sem=ss.at[k_send], recv_sem=rs.at[k_recv],
            device_id=(to_t, to_e), device_id_type=MESH,
        )

    def took(ref, sem):
        pltpu.make_async_copy(ref, ref, sem).wait()

    sent = []

    def to_sibling(src, dst, k):
        remote(src, dst, k, k, t, x * 2 + sib).start()
        sent.append((src, k))

    def fan_a(src, dst, k, total):
        for i in range(1, side):
            to = lax.rem(a + i, side)
            remote(src(to), dst, k, k, to * a_step + b * b_step, e).start()
        sent.append((total, k))

    def fan_b(src, dst, k, total):
        for i in range(1, side):
            to = lax.rem(b + i, side)
            remote(src(to), dst, k, k, a * a_step + to * b_step, e).start()
        sent.append((total, k))

    def fan_x(src, dst, k, total):
        for i in range(1, n_x):
            to = lax.rem(x + i, n_x)
            remote(src(to), dst, k, k, t, to * 2 + core).start()
        sent.append((total, k))

    def sum_of(ref, n):
        total = ref[0].astype(F32)
        for i in range(1, n):
            total += ref[i].astype(F32)
        return total

    barrier = pltpu.get_barrier_semaphore()
    for i in range(1, side):
        for to_t in (lax.rem(a + i, side) * a_step + b * b_step, a * a_step + lax.rem(b + i, side) * b_step):
            pl.semaphore_signal(barrier, inc=1, device_id=(to_t, e), device_id_type=MESH)
    for i in others:
        pl.semaphore_signal(barrier, inc=1, device_id=(t, rel_expert(i)), device_id_type=MESH)

    def local(src, dst, k):
        return pltpu.make_async_copy(src, dst, local_sem.at[k])

    ids_copy = local(ids_hbm, ids.at[0], 0)
    emb_copy = local(emb_hbm.at[:, core], rows.at[b, a], 1)
    small = [
        local(route_hbm, route, 2),
        local(gate_hbm, narrow.at[pl.ds(0, 2)], 3),
        local(labels_hbm, narrow.at[pl.ds(8, tasks)], 4),
        local(tout_hbm, tout, 5),
    ]
    w_in_copy = local(w_in_hbm, w_in, 6)
    w_out_copy = local(w_out_hbm, w_out, 7)
    tin_copy = local(tin_hbm, tin, 8)
    for copy in [emb_copy, ids_copy] + small:
        copy.start()
    emb_copy.wait()
    ids_copy.wait()
    pl.semaphore_wait(barrier, 2 * (side - 1) + n_expert - 1)

    fan_a(lambda to: rows.at[b, a], rows.at[b, a], EMB_A, rows.at[0, pl.ds(0, side - 1)])
    fan_b(lambda to: rows.at[b, a], rows.at[b, a], EMB_B0, rows.at[0, pl.ds(0, side - 1)])
    to_sibling(ids.at[0], ids.at[1], IDS)
    w_in_copy.start()
    w_out_copy.start()
    tin_copy.start()

    for copy in small:
        copy.wait()
    columns = narrow[...].T
    named_by = jnp.concatenate([route[...].astype(F32), jnp.zeros((LANES - 2, batch), F32)], axis=0).T.astype(jnp.int32)
    lane = lax.broadcasted_iota(jnp.int32, (batch, LANES), 1)
    slot_lane = lax.broadcasted_iota(jnp.int32, (batch, slots), 1)
    r0, r1 = named_by[:, 0:1], named_by[:, 1:2]
    gate0, gate1 = columns[:, 0:1], columns[:, 1:2]
    named0, named1 = lane == r0, lane == r1
    named = jnp.where(named0 | named1, 1.0, 0.0).astype(BF16)
    earlier = jnp.where(
        lax.broadcasted_iota(jnp.int32, (batch, batch), 1) < lax.broadcasted_iota(jnp.int32, (batch, batch), 0),
        1.0, 0.0,
    ).astype(BF16)
    before = dot(earlier, named)
    placed = []
    for j, (r, hit) in enumerate(((r0, named0), (r1, named1))):
        pos = jnp.sum(jnp.where(hit, before, 0.0), axis=1, keepdims=True).astype(jnp.int32)
        placed.append(jnp.where(slot_lane == r * cap + pos, 1.0, 0.0))
        place[j] = placed[j].astype(BF16)
        place_both_t[:, j * batch : (j + 1) * batch] = placed[j].T.astype(BF16)
    both = placed[0] + placed[1]
    place_sum[...] = both.astype(BF16)
    place_t[...] = both.T.astype(BF16)

    def code_of(s):
        own = ids[s]
        shard = own // (n_x * 2 * per)
        near = lax.rem(own // (2 * per), n_x) * per + lax.rem(own, per)
        at_a = jnp.where(first, shard // side, lax.rem(shard, side))
        at_b = jnp.where(first, lax.rem(shard, side), shard // side)
        code = jnp.where(lax.rem(own // per, 2) == core, (at_b * side + at_a) * span + near, -1)
        flat = jnp.concatenate([code.astype(F32), jnp.zeros((LANES - lookups, batch), F32)], axis=0)
        return flat.T.astype(jnp.int32)

    def build_counts(s, code, features):
        for f in features:
            words = [jnp.zeros((batch, LANES), jnp.int32) for _ in range(-(-cols // (8 * LANES)))]
            for k in range(bag):
                c = f * bag + k
                gap = code[:, c : c + 1] - lane
                high = gap >> 7
                one = jnp.where(jnp.bitwise_and(gap, LANES - 1) == 0, 1 << (jnp.bitwise_and(high, 7) * 4), 0)
                which = high >> 3
                for w in range(len(words)):
                    words[w] = words[w] + jnp.where(which == w, one, 0)
            for h in range(cols // LANES):
                count = jnp.bitwise_and(words[h // 8] >> (4 * (h % 8)), 15)
                counts[s, f * batch : (f + 1) * batch, h * LANES : (h + 1) * LANES] = count.astype(F32).astype(BF16)

    code = code_of(0)
    early = 3 * n_feat // 4
    build_counts(0, code, range(early))
    took(rows.at[0, pl.ds(0, side - 1)], rs.at[EMB_A])
    for i in range(1, side):
        block = rows.at[b, lax.rem(a + i, side)]
        for j in range(1, side):
            to = lax.rem(b + j, side)
            remote(block, block, EMB_B, EMB_B, a * a_step + to * b_step, e).start()
    sent.append((rows.at[pl.ds(0, side - 1), pl.ds(0, side - 1)], EMB_B))
    build_counts(0, code, range(early, n_feat))
    took(ids.at[1], rs.at[IDS])
    build_counts(1, code_of(1), range(n_feat))

    part_cols = side * span

    def partial(s, c, at_b):
        at = pl.ds(pl.multiple_of(at_b * part_cols, part_cols), part_cols)
        return dot(counts[s, c * CHUNK : (c + 1) * CHUNK, at], rows[at_b].reshape(part_cols, LANES))

    for c in range(n_chunks):
        part_out[c] = partial(1, c, b)
        part_own[c] = partial(0, c, b)
    took(rows.at[0, pl.ds(0, side - 1)], rs.at[EMB_B0])
    took(rows.at[pl.ds(0, side - 1), pl.ds(0, side - 1)], rs.at[EMB_B])

    def all_parts(s, c, total):
        for i in range(1, side):
            total += partial(s, c, lax.rem(b + i, side))
        return total

    def swap_partial(c):
        part_out[c] = all_parts(1, c, part_out[c])
        to_sibling(part_out.at[c], part_in.at[c], PART + c)

    swap_partial(0)
    for c in range(n_chunks):
        mine = all_parts(0, c, part_own[c])
        if c + 1 < n_chunks:
            swap_partial(c + 1)
        took(part_in.at[c], rs.at[PART + c])
        pooled = (mine + part_in[c]).astype(BF16)
        tokens = jnp.concatenate([pooled[f * batch : (f + 1) * batch] for f in range(per_chunk)], axis=1)
        outbox[c] = dot(place_t[...], tokens).astype(BF16).reshape(n_expert, cap, CHUNK)
        for i in others:
            to = rel_expert(i)
            remote(outbox.at[c, to], inbox.at[c, rel_back(i)], BOX + c, BOX + c, t, to).start()
        sent.append((outbox.at[c, pl.ds(0, n_expert - 1)], BOX + c))
        inbox[c, me] = outbox[c, e]

    w_in_copy.wait()
    w_out_copy.wait()

    def arrived(half):
        return pl.ds(half * rel_per, rel_per - (me // rel_per == half))

    tile = min(TILE, hid)

    for c in range(n_chunks - 1):
        took(inbox.at[c, pl.ds(0, n_expert - 1)], rs.at[BOX + c])

        @pl.loop(0, hid // tile)
        def _(n):
            at = pl.ds(pl.multiple_of(n * tile, tile), tile)
            pre = dot(inbox[c].reshape(slots, CHUNK), w_in[c * CHUNK : (c + 1) * CHUNK, at])
            pre_acc[:, at] = pre if c == 0 else pre_acc[:, at] + pre

    last = n_chunks - 1
    took(inbox.at[last, pl.ds(0, n_expert - 1)], rs.at[BOX + last])
    for half in range(HALVES):
        acc[...] = jnp.zeros_like(acc)
        mine = slice(half * rel_per, (half + 1) * rel_per)

        @pl.loop(0, hid // tile)
        def _(n):
            at = pl.ds(pl.multiple_of(n * tile, tile), tile)
            pre = dot(inbox[last, mine].reshape(m_rows, CHUNK), w_in[last * CHUNK : (last + 1) * CHUNK, at])
            pre += pre_acc[half * m_rows : (half + 1) * m_rows, at]
            hidden, grad = silu_and_slope(pre)
            slope[half, :, at] = grad.astype(BF16)
            acc[...] += dot(hidden.astype(BF16), w_out[at, :])

        made[mine] = acc[...].astype(BF16).reshape(rel_per, cap, eout)
        for i in others:
            if i // rel_per == half:
                remote(made.at[i], returned.at[e], BACK, BACK, t, rel_expert(i)).start()

    sent.append((made.at[pl.ds(0, n_expert - 1)], BACK))
    returned[e] = made[me]
    tin_copy.wait()
    took(returned.at[pl.ds(0, n_expert - 1)], rs.at[BACK])

    answers = returned[...].reshape(slots, eout)
    both = dot(place[...].reshape(2 * batch, slots), answers)
    combined = (gate0 * both[:batch] + gate1 * both[batch:]).astype(BF16)
    comb[0] = combined
    per_half = tasks // 2
    for k in range(tasks):
        pre = dot(combined, tin[:, k * tw : (k + 1) * tw])
        units, unit_slope = silu_and_slope(pre)
        out_row = tout[k : k + 1, :]
        logit = jnp.sum(units * out_row, axis=1, keepdims=True)
        dlogit = (jax.nn.sigmoid(logit) - columns[:, 8 + k : 9 + k]) / tasks
        gto_out[0, k : k + 1, :] = jnp.sum(dlogit * units, axis=0, keepdims=True)
        grad = (dlogit * out_row * unit_slope).astype(BF16)
        dtow[k // per_half, :, (k % per_half) * tw : (k % per_half + 1) * tw] = grad
    to_sibling(comb.at[0], comb.at[1], COMB)
    to_sibling(dtow.at[sib], dtow_own.at[1], DTOW)
    dcomb = sum(dot_nt(dtow[h], tin[:, h * per_half * tw : (h + 1) * per_half * tw]) for h in range(2))
    dent = jnp.concatenate([(gate0 * dcomb).astype(BF16), (gate1 * dcomb).astype(BF16)], axis=0)
    dout[...] = dot(place_both_t[...], dent).astype(BF16).reshape(n_expert, cap, eout)
    for i in others:
        at = rel_back(i)
        to = rel_expert(i)
        remote(dout.at[to], din.at[at], DBOX, DBOX + at // rel_per, t, to).start()
    sent.append((dout.at[pl.ds(0, n_expert - 1)], DBOX))
    din[me] = dout[e]

    fan_a(lambda to: gto_out.at[0], gto_a.at[a], GTO_A, gto_a.at[pl.ds(0, side - 1)])
    gto_a[a] = gto_out[0]
    dtow_own[0] = dtow[core]
    comb_t[:, 0:batch] = comb[0].astype(F32).T.astype(BF16)
    took(comb.at[1], rs.at[COMB])
    took(dtow_own.at[1], rs.at[DTOW])
    comb_t[:, batch : 2 * batch] = comb[1].astype(F32).T.astype(BF16)
    t_rows = eout // n_table
    t_cols = tasks * tw // 2
    big = side * t_rows

    @pl.loop(0, side)
    def _(i):
        block = dot(comb_t[pl.ds(pl.multiple_of(i * big, big), big), :], dtow_own[...].reshape(2 * batch, t_cols))
        tower_a_out[i] = block.astype(BF16)

    fan_a(lambda to: tower_a_out.at[to], tower_a_in.at[a], TOW_A, tower_a_in.at[pl.ds(0, side - 1)])
    tower_a_in[a] = tower_a_out[a]

    n_wide = width // WIDE

    def token_grads(half, c):
        block = dot_nt(slope[half], w_in[c * WIDE : (c + 1) * WIDE, :])
        drows[c, half * rel_per : (half + 1) * rel_per] = block.astype(BF16).reshape(rel_per, cap, WIDE)
        for i in others:
            if i // rel_per == half:
                remote(drows.at[c, i], dback.at[c, e], DBACK + c, DBACK + c, t, rel_expert(i)).start()

    def tower_first():
        took(tower_a_in.at[pl.ds(0, side - 1)], rs.at[TOW_A])
        took(gto_a.at[pl.ds(0, side - 1)], rs.at[GTO_A])
        tower_b_out[...] = sum_of(tower_a_in, side).astype(BF16).reshape(side, t_rows, t_cols)
        fan_b(lambda to: tower_b_out.at[to], tower_b_in.at[b], TOW_B, tower_b_in.at[pl.ds(0, side - 1)])
        tower_b_in[b] = tower_b_out[b]
        gto_out[1] = sum_of(gto_a, side)
        fan_b(lambda to: gto_out.at[1], gto_b.at[b], GTO_B, gto_b.at[pl.ds(0, side - 1)])
        gto_b[b] = gto_out[1]

    for half in range(HALVES):
        took(din.at[arrived(half)], rs.at[DBOX + half])
        if half == HALVES - 1:
            tower_first()
        mine = slice(half * rel_per, (half + 1) * rel_per)

        @pl.loop(0, hid // tile)
        def _(n):
            at = pl.ds(pl.multiple_of(n * tile, tile), tile)
            dhid = dot_nt(din[mine].reshape(m_rows, eout), w_out[at, :])
            slope[half, :, at] = (dhid * slope[half, :, at].astype(F32)).astype(BF16)

        for c in range(n_wide):
            token_grads(half, c)

    for c in range(n_wide):
        dback[c, e] = drows[c, me]
        sent.append((drows.at[c, pl.ds(0, n_expert - 1)], DBACK + c))

    def pooled_grads(c):
        took(dback.at[c, pl.ds(0, n_expert - 1)], rs.at[DBACK + c])
        got = dot(place_sum[...], dback[c].reshape(slots, WIDE)).astype(BF16).astype(F32)
        for f in range(WIDE // LANES):
            dpooled_t[c, 0, :, f * batch : (f + 1) * batch] = got[:, f * LANES : (f + 1) * LANES].T.astype(BF16)
        to_sibling(dpooled_t.at[c, 0], dpooled_t.at[c, 1], DPOOL + c)

    def row_grads(c, s, at_a):
        parts = [
            counts[s, c * WIDE : (c + 1) * WIDE, pl.ds(pl.multiple_of((bb * side + at_a) * span, span), span)]
            for bb in range(side)
        ]
        return dot(dpooled_t[c, s], jnp.concatenate(parts, axis=1))

    def add_chunk(c, s):
        if s == 1:
            took(dpooled_t.at[c, 1], rs.at[DPOOL + c])
        for at_a in range(side):
            part = row_grads(c, s, at_a)
            grad_acc[at_a] = part if c == 0 and s == 0 else grad_acc[at_a] + part

    def gin_rows(at, n):
        return pl.ds(pl.multiple_of(at * t_rows, t_rows), n * t_rows)

    x_cols = t_cols // n_x // 2
    g_cols = t_cols // 2
    x_at = pl.ds(pl.multiple_of(x * x_cols, x_cols), x_cols)
    my_rows, my_big = gin_rows(a * side + b, 1), gin_rows(a * side, side)
    from_b = gin.at[0, :, pl.ds(0, (side - 1) * t_rows), pl.ds(0, x_cols)]
    from_x = gin.at[0, 0, pl.ds(0, side * t_rows), pl.ds(0, (n_x - 1) * x_cols)]
    from_a = gin.at[0, 0, pl.ds(0, (side - 1) * side * t_rows), pl.ds(0, x_cols)]
    from_far_x = gin.at[0, 0, :, pl.ds(0, (n_x - 1) * x_cols)]

    def tower_second():
        took(tower_b_in.at[pl.ds(0, side - 1)], rs.at[TOW_B])
        took(gto_b.at[pl.ds(0, side - 1)], rs.at[GTO_B])
        total = sum_of(tower_b_in, side)
        for k in range(n_x):
            for h in range(2):
                at = h * g_cols + k * x_cols
                tower_x_out[k, h] = total[:, at : at + x_cols].astype(BF16)
        fan_x(lambda to: tower_x_out.at[to], tower_x_in.at[x], TOW_X, tower_x_in.at[pl.ds(0, n_x - 1)])
        tower_x_in[x] = tower_x_out[x]
        gto_out[2] = sum_of(gto_b, side)
        for i in others:
            remote(gto_out.at[2], gto_e.at[e], GTO_E, GTO_E, t, rel_expert(i)).start()
        sent.append((gto_e.at[pl.ds(0, n_expert - 1)], GTO_E))
        gto_e[e] = gto_out[2]

    def tower_x():
        took(tower_x_in.at[pl.ds(0, n_x - 1)], rs.at[TOW_X])
        gin[core, :, my_rows, x_at] = sum_of(tower_x_in, n_x).astype(BF16)
        block = gin.at[core, :, my_rows, x_at]
        fan_b(lambda to: block, block, GIN_B, from_b)

    def gather_b():
        took(from_b, rs.at[GIN_B])
        near = gin.at[core, 1, my_big, x_at]
        fan_a(lambda to: near, near, GIN_A2, from_a)
        block = gin.at[core, 0, my_big, x_at]
        fan_x(lambda to: block, block, GIN_X, from_x)

    gin_outs = []

    def gin_out(half, h, at):
        to = pl.ds(pl.multiple_of(half * t_cols + h * g_cols, g_cols), g_cols)
        copy = local(gin.at[half, h, at], gin_hbm.at[at, to], 9 + len(gin_outs))
        copy.start()
        gin_outs.append(copy)

    def whole(i):
        at = gin_rows(lax.rem(a + i, side) * side, side)
        block = gin.at[core, 0, at]
        to_sibling(block, block, GIN_S + i)
        gin_out(core, 0, at)

    def gather_x():
        took(from_x, rs.at[GIN_X])
        block = gin.at[core, 0, my_big]
        for i in range(1, side):
            to = lax.rem(a + i, side)
            remote(block, block, GIN_A + i, GIN_A + side - i, to * a_step + b * b_step, e).start()
            sent.append((block, GIN_A + i))
        whole(0)

    def gather_far():
        took(from_a, rs.at[GIN_A2])
        block = gin.at[core, 1, :, x_at]
        fan_x(lambda to: block, block, GIN_X2, from_far_x)

    def gather_a(i):
        took(gin.at[0, 0, my_big], rs.at[GIN_A + i])
        whole(i)

    def gather_far_x():
        took(from_far_x, rs.at[GIN_X2])
        block = gin.at[core, 1]
        to_sibling(block, block, GIN_S2)
        gin_out(core, 1, pl.ds(0, eout))

    def from_sibling(i):
        took(gin.at[0, 0, my_big], rs.at[GIN_S + i])
        gin_out(sib, 0, gin_rows(lax.rem(b + i, side) * side, side))

    def far_from_sibling():
        took(gin.at[0, 1], rs.at[GIN_S2])
        gin_out(sib, 1, pl.ds(0, eout))

    tower_second()
    last = n_wide - 1
    for c in range(n_wide):
        pooled_grads(c)
        if c > 0:
            add_chunk(c - 1, 1)
            tower_x()
        if c < last:
            add_chunk(c, 0)
    took(dpooled_t.at[last, 1], rs.at[DPOOL + last])
    for i in range(1, side):
        to = lax.rem(a + i, side)
        ga_out[to] = (grad_acc[to] + row_grads(last, 0, to) + row_grads(last, 1, to)).astype(BF16)
        remote(ga_out.at[to], ga_in.at[a], GRAD_A, GRAD_A, to * a_step + b * b_step, e).start()
    sent.append((ga_in.at[pl.ds(0, side - 1)], GRAD_A))
    ga_in[a] = (grad_acc[a] + row_grads(last, 0, a) + row_grads(last, 1, a)).astype(BF16)

    gather_b()
    gather_x()
    took(ga_in.at[pl.ds(0, side - 1)], rs.at[GRAD_A])
    total = sum_of(ga_in, side)
    for k in range(side):
        gb_out[k] = total[:, k * span : (k + 1) * span].astype(BF16)
    fan_b(lambda to: gb_out.at[to], gb_in.at[b], GRAD_B, gb_in.at[pl.ds(0, side - 1)])
    gb_in[b] = gb_out[b]
    gather_far()
    took(gto_e.at[pl.ds(0, n_expert - 1)], rs.at[GTO_E])
    gtout[...] = sum_of(gto_e, n_expert)
    gto_copy = local(gtout, gtout_hbm, 11 + 2 * side)
    gto_copy.start()
    took(gb_in.at[pl.ds(0, side - 1)], rs.at[GRAD_B])
    gx_out[...] = sum_of(gb_in, side).T.astype(BF16).reshape(n_x, per, LANES)
    fan_x(lambda to: gx_out.at[to], gx_in.at[x], GRAD_X, gx_in.at[pl.ds(0, n_x - 1)])
    gx_in[x] = gx_out[x]
    for i in range(1, side):
        gather_a(i)
    gather_far_x()
    took(gx_in.at[pl.ds(0, n_x - 1)], rs.at[GRAD_X])
    grows[...] = sum_of(gx_in, n_x)
    grows_copy = local(grows, grows_hbm, 12 + 2 * side)
    grows_copy.start()
    for i in range(side):
        from_sibling(i)
    far_from_sibling()

    for ref, k in sent:
        took(ref, ss.at[k])
    for copy in gin_outs + [gto_copy, grows_copy]:
        copy.wait()


def finish(gin_hbm, grows_hbm, gto_hbm, gin_out, grows_out, gto_out, narrow, wide, sem_in, sem_out):
    n = sem_in.shape[0] - 2
    step = narrow.shape[0] // n
    pieces = [pl.ds(i * step, step) for i in range(n)]
    ins = [pltpu.make_async_copy(gin_hbm.at[p], narrow.at[p], sem_in.at[i]) for i, p in enumerate(pieces)]
    outs = [pltpu.make_async_copy(wide.at[p], gin_out.at[p], sem_out.at[i]) for i, p in enumerate(pieces)]
    small = [
        pltpu.make_async_copy(grows_hbm, grows_out, sem_in.at[n]),
        pltpu.make_async_copy(gto_hbm, gto_out, sem_in.at[n + 1]),
    ]
    for copy in ins + small:
        copy.start()
    for i, p in enumerate(pieces):
        ins[i].wait()
        wide[p] = narrow[p].astype(F32)
        outs[i].start()
    for copy in outs + small:
        copy.wait()


def per_device(emb_rows, row_ids, route_ids, route_gates, w_in, w_out, tower_in, tower_out, labels):
    n_table = lax.axis_size("table")
    n_expert = lax.axis_size("expert")
    n_x = n_expert // 2
    side = math.isqrt(n_table)
    samples, tables, bag = row_ids.shape
    cap = 3 * samples // n_expert
    row_dev, dim = emb_rows.shape
    width = tables * dim
    hid, eout = w_out.shape[1:]
    tasks, tw = tower_out.shape
    per = row_dev // n_expert
    span = n_x * per
    cols = n_table * span
    slots = n_expert * cap
    n_chunks = width // CHUNK
    m_rows = slots // HALVES
    t_rows = eout // n_table
    t_cols = tasks * tw // 2
    x_cols = t_cols // n_x // 2
    n_wide = width // WIDE
    hbm = pl.BlockSpec(memory_space=pl.ANY)
    dma = pltpu.SemaphoreType.DMA
    scratch = [
        pltpu.VMEM((width, hid), BF16),
        pltpu.VMEM((hid, eout), BF16),
        pltpu.VMEM((eout, tasks * tw), BF16),
        pltpu.VMEM((2, tables * bag, samples), jnp.int32),
        pltpu.VMEM((2, samples), jnp.int32),
        pltpu.VMEM((LANES, samples), F32),
        pltpu.VMEM((tasks, tw), F32),
        pltpu.VMEM((per, dim), F32),
        pltpu.VMEM((tasks, tw), F32),
        pltpu.VMEM((2, width, cols), BF16),
        pltpu.VMEM((side, side, n_x, per, LANES), BF16),
        pltpu.VMEM((n_chunks, CHUNK, LANES), F32),
        pltpu.VMEM((n_chunks, CHUNK, LANES), F32),
        pltpu.VMEM((n_chunks, CHUNK, LANES), F32),
        pltpu.VMEM((2, samples, slots), BF16),
        pltpu.VMEM((samples, slots), BF16),
        pltpu.VMEM((slots, samples), BF16),
        pltpu.VMEM((slots, 2 * samples), BF16),
        pltpu.VMEM((n_chunks, n_expert, cap, CHUNK), BF16),
        pltpu.VMEM((n_chunks, n_expert, cap, CHUNK), BF16),
        pltpu.VMEM((m_rows, eout), F32),
        pltpu.VMEM((slots, hid), F32),
        pltpu.VMEM((HALVES, m_rows, hid), BF16),
        pltpu.VMEM((n_expert, cap, eout), BF16),
        pltpu.VMEM((n_expert, cap, eout), BF16),
        pltpu.VMEM((2, samples, eout), BF16),
        pltpu.VMEM((2, samples, t_cols), BF16),
        pltpu.VMEM((2, samples, t_cols), BF16),
        pltpu.VMEM((eout, 2 * samples), BF16),
        pltpu.VMEM((side, side * t_rows, t_cols), BF16),
        pltpu.VMEM((side, side * t_rows, t_cols), BF16),
        pltpu.VMEM((side, t_rows, t_cols), BF16),
        pltpu.VMEM((side, t_rows, t_cols), BF16),
        pltpu.VMEM((n_x, 2, t_rows, x_cols), BF16),
        pltpu.VMEM((n_x, 2, t_rows, x_cols), BF16),
        pltpu.VMEM((2, 2, eout, t_cols // 2), BF16),
        pltpu.VMEM((3, tasks, tw), F32),
        pltpu.VMEM((side, tasks, tw), F32),
        pltpu.VMEM((side, tasks, tw), F32),
        pltpu.VMEM((n_expert, tasks, tw), F32),
        pltpu.VMEM((n_expert, cap, eout), BF16),
        pltpu.VMEM((n_expert, cap, eout), BF16),
        pltpu.VMEM((n_wide, n_expert, cap, WIDE), BF16),
        pltpu.VMEM((n_wide, n_expert, cap, WIDE), BF16),
        pltpu.VMEM((n_wide, 2, LANES, WIDE), BF16),
        pltpu.VMEM((side, LANES, side * span), F32),
        pltpu.VMEM((side, LANES, side * span), BF16),
        pltpu.VMEM((side, LANES, side * span), BF16),
        pltpu.VMEM((side, LANES, span), BF16),
        pltpu.VMEM((side, LANES, span), BF16),
        pltpu.VMEM((n_x, per, LANES), BF16),
        pltpu.VMEM((n_x, per, LANES), BF16),
        dma((13 + 2 * side,)),
        dma((N_SEMS,)),
        dma((N_SEMS,)),
    ]
    grows, gin, gtout = pl.pallas_call(
        functools.partial(kernel, n_table, n_expert),
        out_shape=(
            jax.ShapeDtypeStruct((per, dim), F32),
            jax.ShapeDtypeStruct((eout, tasks * tw), BF16),
            jax.ShapeDtypeStruct((tasks, tw), F32),
        ),
        in_specs=[hbm] * 9,
        out_specs=(hbm,) * 3,
        scratch_shapes=scratch,
        compiler_params=pltpu.CompilerParams(
            collective_id=0, has_side_effects=True, vmem_limit_bytes=VMEM_LIMIT
        ),
    )(
        jnp.transpose(row_ids, (1, 2, 0)).reshape(tables * bag, samples),
        emb_rows.reshape(n_x, 2, per, dim),
        route_ids.T,
        route_gates.T,
        labels.T,
        tower_out,
        w_in[0],
        w_out[0],
        tower_in,
    )
    gin, grows, gtout = pl.pallas_call(
        finish,
        out_shape=(
            jax.ShapeDtypeStruct((eout, tasks * tw), F32),
            jax.ShapeDtypeStruct((per, dim), F32),
            jax.ShapeDtypeStruct((tasks, tw), F32),
        ),
        in_specs=[hbm] * 3,
        out_specs=(hbm,) * 3,
        scratch_shapes=[
            pltpu.VMEM((eout, tasks * tw), BF16),
            pltpu.VMEM((eout, tasks * tw), F32),
            dma((10,)),
            dma((8,)),
        ],
    )(gin, grows, gtout)
    return grows, gin, gtout


VMEM_LIMIT = 63 * 1024 * 1024


def solution(mesh):
    return jax.shard_map(
        per_device,
        mesh=mesh,
        in_specs=(
            P("table", None),
            P(("table", "expert"), None, None),
            P(("table", "expert"), None),
            P(("table", "expert"), None),
            P("expert", None, None),
            P("expert", None, None),
            P(),
            P(),
            P(("table", "expert"), None),
        ),
        out_specs=(P(("table", "expert"), None), P(), P()),
        check_vma=False,
    )
```
